32 devices in a mesh: row: 8 (over z, x), reach: 4 (over y, core).
Axes of the slice: x: 2, y: 2, z: 4, core: 2. Of those that a mesh axis runs over, the one named last changes fastest.
Arguments:
- basis: bfloat16 [65536, 128], P(('row', 'reach')), may hold values from -6 to 6
- near_cols: int32 [1024, 7], P(('row', 'reach')), may hold values from 0 to 127, as said below
- near_count: int32 [1024], P(('row', 'reach')), may hold values from 1 to 7
- near_blocks: bfloat16 [1024, 7, 4096], P(('row', 'reach')), may hold values from -0.25 to 0.25
- marker_rows: int32 [512], P(('row', 'reach')), may hold values from 0 to 31
- marker_groups: int32 [512], P(('row', 'reach')), may hold values from 0 to 63, as said below
- marker_count: int32 [32], P(('row', 'reach')), may hold values from 2 to 16
- marker_weights: bfloat16 [512, 4096], P(('row', 'reach')), may hold values from -0.75 to 0.75
- stiffness: float32 [4096], replicated, may hold values from 0.5 to 4
Outputs:
- qfactor: float32 [65536, 128], P(('row', 'reach'))
- rfactor: float32 [128, 128], replicated
The draws below stay inside these ranges and needn't reach their ends.
Inputs may be any that keep to these rules, and one draw needn't show every extreme that they name: `near_cols`: the first stored block of each block row is the block row itself. `marker_groups`: slot 0 of slab s names group ((64 * s) // 32 + 64 // 2) % 64; slot 1 names (64 * s) // 32; every other slot names that group or the one after it, never beyond 64 - 1.
All inputs are finite; a program needn't handle non-finite values.
Results may differ from the reference program's by a relative error of at most 0.0025.
Values may be sent and summed in bfloat16 or wider, within the bound.
A program may use at most 64 MiB of HBM per device.

```python
import math
import jax
import jax.numpy as jnp
from jax import lax

BS = 64
COLS = 128
NB = 7
SB = 32
MB = 16
NG = 64
NDEV = 32
REACH_BLK = 128
NBLK = 1024
ROWS = 65536
MARKERS = 512
NM = 4096
N_REACH = 4


def draw_near_cols(key, part):
    picks = jax.random.randint(key, (NBLK, NB - 1), 0, REACH_BLK, dtype=jnp.int32)
    own = (jnp.arange(NBLK, dtype=jnp.int32) % REACH_BLK)[:, None]
    return jnp.concatenate([own, picks], axis=1).astype(jnp.int32)


def draw_near_count(key, part):
    counts = jax.random.randint(key, (NBLK,), 1, NB + 1, dtype=jnp.int32)
    full = jnp.arange(NBLK, dtype=jnp.int32) % SB == 0
    return jnp.where(full, NB, counts).astype(jnp.int32)


def draw_marker_groups(key, part):
    slot = jnp.arange(MARKERS, dtype=jnp.int32)
    within = slot % MB
    base = slot // MB * NG // NDEV
    step = jax.random.randint(key, (MARKERS,), 0, 2, dtype=jnp.int32)
    step = jnp.where(within == 1, 0, step)
    near_group = jnp.minimum(base + step, NG - 1)
    far_group = (base + NG // 2) % NG
    return jnp.where(within == 0, far_group, near_group).astype(jnp.int32)


def draw_marker_count(key, part):
    slab = jnp.arange(NDEV, dtype=jnp.int32)
    light = jax.random.randint(key, (NDEV,), 2, max(MB // 2, 3) + 1, dtype=jnp.int32)
    return jnp.where(slab % 8 < 2, MB, light).astype(jnp.int32)


def set_ends(drawn, rng, smallest, top_value):
    longest = drawn.shape.index(max(drawn.shape))
    spots = []
    for shift in (0, 1):
        where = [jax.random.randint(jax.random.fold_in(rng, axis), (), 0, length) for axis, length in enumerate(drawn.shape)]
        where[longest] = (where[longest] + shift) % drawn.shape[longest]
        spots.append(tuple(where))
    return drawn.at[spots[0]].set(smallest).at[spots[1]].set(top_value)


def steps_of(key, extent, split, smallest, high):
    factor_of, own = 1.0, jax.random.fold_in(key, 6)
    for axis_at, blocks in split:
        heights = jnp.exp(jax.random.uniform(jax.random.fold_in(own, axis_at), (blocks,), jnp.float32, smallest / len(split), high / len(split)))
        factor_of = factor_of * jnp.repeat(heights, extent[axis_at] // blocks).reshape([-1 if axis == axis_at else 1 for axis in range(len(extent))])
    return factor_of


def gaussian(stream_key, extent, scale, limit, cuts=(), kind=jnp.bfloat16):
    gain = steps_of(stream_key, extent, cuts, -0.22, 0.18) if cuts else 1.0
    entries = jax.random.normal(stream_key, extent, jnp.float32) * scale * gain
    return jnp.minimum(jnp.maximum(entries, -limit), limit).astype(kind)


def setup_inputs(seed: int = 0) -> dict:
    splits = jax.random.split(jax.random.key(seed), 10)
    basis = gaussian(splits[0], (ROWS, COLS), 1.0, 6.0, ((0, 32),))
    near_cols = draw_near_cols(jax.random.fold_in(splits[9], 71), 0)
    near_count = draw_near_count(jax.random.fold_in(splits[9], 71), 0)
    near_blocks = gaussian(splits[3], (NBLK, NB, BS * BS), (NB * BS) ** -0.5, 0.25, ((0, 32),))
    marker_rows = set_ends(jax.random.randint(splits[4], (MARKERS,), 0, SB), jax.random.fold_in(splits[4], 1), 0, SB - 1).astype(jnp.int32)
    marker_groups = draw_marker_groups(jax.random.fold_in(splits[9], 71), 0)
    marker_count = draw_marker_count(jax.random.fold_in(splits[9], 71), 0)
    marker_weights = gaussian(splits[7], (MARKERS, BS * BS), BS ** -0.5, 0.75, ((0, 32),))
    stiffness = jnp.clip(jnp.exp(jax.random.uniform(splits[8], (NM,), jnp.float32, math.log(0.5), math.log(4.0))), 0.5, 4.0)
    return {"basis": basis, "near_cols": near_cols, "near_count": near_count, "near_blocks": near_blocks, "marker_rows": marker_rows, "marker_groups": marker_groups, "marker_count": marker_count, "marker_weights": marker_weights, "stiffness": stiffness}


def force_of(sums, stiffness):
    scale = lax.rsqrt(1.0 + lax.optimization_barrier(jnp.mean(sums * sums, axis=1, keepdims=True)))
    return (stiffness[:, None] * sums * scale).astype(jnp.bfloat16)

def reference(basis, near_cols, near_count, near_blocks, marker_rows, marker_groups, marker_count, marker_weights, stiffness):
    slab_rows = SB * BS
    hp = lax.Precision.HIGHEST

    def slab_terms(dev):
        own = lax.dynamic_slice_in_dim(basis, (dev * slab_rows).astype(jnp.int32), slab_rows, 0).reshape(SB, BS, COLS)
        mrows = lax.dynamic_slice_in_dim(marker_rows, (dev * MB).astype(jnp.int32), MB, 0)
        mgroups = lax.dynamic_slice_in_dim(marker_groups, (dev * MB).astype(jnp.int32), MB, 0)
        weights = lax.dynamic_slice_in_dim(marker_weights, (dev * MB).astype(jnp.int32), MB, 0).reshape(MB, BS, BS)
        mlive = jnp.arange(MB, dtype=jnp.int32) < marker_count[dev]
        return (own, mrows, mgroups, weights, mlive)

    def interp(total, dev):
        own, mrows, mgroups, weights, mlive = slab_terms(dev)
        picked = own[mrows].astype(jnp.float32)
        partial_value = jnp.einsum('mcj,mcd->mjd', weights.astype(jnp.float32), picked, precision=hp)
        onehot = ((mgroups[None, :] == jnp.arange(NG, dtype=jnp.int32)[:, None]) & mlive[None, :]).astype(jnp.float32)
        return (total + jnp.dot(onehot, partial_value.reshape(MB, BS * COLS), precision=hp), None)
    gathered, _ = lax.scan(interp, jnp.zeros((NG, BS * COLS), jnp.float32), jnp.arange(NDEV, dtype=jnp.int32))
    force = force_of(gathered.reshape(NM, COLS), stiffness).reshape(NG, BS, COLS)

    def slab_image(dev):
        own, mrows, mgroups, weights, mlive = slab_terms(dev)
        group_start = dev // N_REACH * REACH_BLK * BS
        group = lax.dynamic_slice_in_dim(basis, group_start.astype(jnp.int32), REACH_BLK * BS, 0).reshape(REACH_BLK, BS, COLS)
        cols = lax.dynamic_slice_in_dim(near_cols, (dev * SB).astype(jnp.int32), SB, 0)
        count = lax.dynamic_slice_in_dim(near_count, (dev * SB).astype(jnp.int32), SB, 0)
        blocks = lax.dynamic_slice_in_dim(near_blocks, (dev * SB).astype(jnp.int32), SB, 0).reshape(SB, NB, BS, BS)
        live = jnp.arange(NB, dtype=jnp.int32)[None, :] < count[:, None]
        fetched = jnp.where(live[:, :, None, None], group[cols], jnp.zeros((), jnp.bfloat16))
        near = jnp.einsum('bkrc,bkcd->brd', blocks.astype(jnp.float32), fetched.astype(jnp.float32), precision=hp)
        fm = jnp.where(mlive[:, None, None], force[mgroups], jnp.zeros((), jnp.bfloat16))
        contrib = jnp.einsum('mcj,mjd->mcd', weights.astype(jnp.float32), fm.astype(jnp.float32), precision=hp)
        rowhot = ((mrows[None, :] == jnp.arange(SB, dtype=jnp.int32)[:, None]) & mlive[None, :]).astype(jnp.float32)
        spread = jnp.dot(rowhot, contrib.reshape(MB, BS * COLS), precision=hp).reshape(SB, BS, COLS)
        return (near + spread).reshape(slab_rows, COLS)
    image = lax.map(slab_image, jnp.arange(NDEV, dtype=jnp.int32)).reshape(ROWS, COLS)
    gram = jnp.dot(image.T, image, precision=hp)
    lower = jnp.linalg.cholesky(gram)
    solved = jax.scipy.linalg.solve_triangular(lower, image.T, lower=True)
    root = jnp.sqrt(jnp.float32(ROWS))
    return (solved.T * root, lower.T / root)
```

```python
import functools

import jax
import jax.numpy as jnp
from jax import lax
from jax.experimental import pallas as pl
from jax.experimental.pallas import tpu as pltpu
from jax.sharding import PartitionSpec as P

BS = 64
NG = 64
CHUNKS = 4
HP = lax.Precision.HIGHEST
MESH = pl.DeviceIdType.MESH
VM = pl.BlockSpec(memory_space=pltpu.VMEM)
SM = pl.BlockSpec(memory_space=pltpu.SMEM)


def dot(a, b, da, db, precision=None):
    return lax.dot_general(
        a, b, (((da,), (db,)), ((), ())), precision=precision, preferred_element_type=jnp.float32
    )


def image_kernel(
    rows,
    reach,
    cols,
    mrow,
    code,
    basis,
    blocks,
    weights,
    stiff,
    image,
    gram,
    grp,
    sums,
    other,
    force,
    contrib,
    part,
    buf1,
    quarter,
    buf2,
    local_sem,
    sib_send,
    sib_recv,
    y_send,
    y_recv,
    f_send,
    f_recv,
    m_send,
    m_recv,
    s1,
    r1,
    s2,
    r2,
    s3,
    r3,
):
    z = lax.axis_index("row")
    r = lax.axis_index("reach")
    slab, side, width = basis.shape
    stored = blocks.shape[2] // side
    slots = weights.shape[0]
    core = lax.rem(r, 2)
    sib = r + 1 - 2 * core
    far = lax.rem(r + 2, reach)

    barrier = pltpu.get_barrier_semaphore()
    for d in range(1, reach):
        pl.semaphore_signal(
            barrier, inc=1, device_id=(z, lax.rem(r + d, reach)), device_id_type=MESH
        )
    for d in range(1, rows):
        pl.semaphore_signal(
            barrier, inc=1, device_id=(lax.rem(z + d, rows), r), device_id_type=MESH
        )
    pl.semaphore_wait(barrier, reach + rows - 2)

    def remote(src, dst, ss, rs, dev):
        return pltpu.make_async_remote_copy(
            src_ref=src, dst_ref=dst, send_sem=ss, recv_sem=rs, device_id=dev, device_id_type=MESH
        )

    step = slab // CHUNKS
    to_far = []
    for c in range(CHUNKS):
        cp = remote(
            basis.at[pl.ds(c * step, step)],
            grp.at[pl.ds(r * slab + c * step, step)],
            y_send.at[c],
            y_recv.at[c],
            (z, far),
        )
        cp.start()
        to_far.append(cp)
    to_sib = remote(basis, grp.at[pl.ds(r * slab, slab)], sib_send, sib_recv, (z, sib))
    to_sib.start()
    own = pltpu.make_async_copy(basis, grp.at[pl.ds(r * slab, slab)], local_sem)
    own.start()
    grp[reach * slab] = jnp.zeros((side, width), grp.dtype)

    sums[...] = jnp.zeros_like(sums)

    def gather_step(m, carry):
        value = dot(weights[m], basis[mrow[m]], 0, 0)
        for g in range(3):
            sums[g] = sums[g] + jnp.where(code[m] == g, 1.0, 0.0) * value
        return carry

    lax.fori_loop(0, slots, gather_step, 0)
    swap = remote(
        sums.at[pl.ds(0, 2)], other, m_send, m_recv, (lax.rem(z + rows // 2, rows), r)
    )
    swap.start()

    def force_of(total, g):
        scale = lax.rsqrt(1.0 + jnp.mean(total * total, axis=1, keepdims=True))
        return (stiff[g] * total * scale).astype(jnp.bfloat16)

    force[2] = force_of(sums[2], 2)
    fwd = []
    for c in range(CHUNKS):
        to_far[c].wait_recv()
        place = pl.ds(far * slab + c * step, step)
        cp = remote(grp.at[place], grp.at[place], f_send.at[c], f_recv.at[c], (z, sib))
        cp.start()
        fwd.append(cp)
    swap.wait()
    force[0] = force_of(sums[0] + other[1], 0)
    force[1] = force_of(sums[1] + other[0], 1)

    def spread_step(m, carry):
        contrib[m] = dot(weights[m], force[jnp.minimum(code[m], 2)], 1, 0)
        return carry

    lax.fori_loop(0, slots, spread_step, 0)

    own.wait()
    to_sib.wait()
    for c in range(CHUNKS):
        to_far[c].wait_send()
        fwd[c].wait()

    def near_step(i, carry):
        fetched = jnp.concatenate([grp[cols[i * stored + k]] for k in range(stored)], axis=0)
        acc = dot(blocks[i], fetched, 1, 0)
        for m in range(slots):
            hit = jnp.where((mrow[m] == i) & (code[m] < 3), 1.0, 0.0)
            acc = acc + hit * contrib[m]
        image[pl.ds(pl.multiple_of(i * side, side), side)] = acc
        return carry

    lax.fori_loop(0, slab, near_step, 0)

    part[...] = jnp.zeros_like(part)

    def gram_step(i, carry):
        x = image[pl.ds(pl.multiple_of(i * 256, 256), 256)]
        part[...] += dot(x, x, 0, 0, HP).reshape(part.shape)
        return carry

    lax.fori_loop(0, slab * side // 256, gram_step, 0)

    first = []
    for d in range(1, reach):
        peer = lax.rem(r + d, reach)
        cp = remote(part.at[peer], buf1.at[d - 1], s1.at[d - 1], r1.at[d - 1], (z, peer))
        cp.start()
        first.append(cp)
    for cp in first:
        cp.wait()
    total = part[r]
    for d in range(reach - 1):
        total = total + buf1[d]
    quarter[...] = total
    second = []
    for d in range(1, rows):
        peer = lax.rem(z + d, rows)
        cp = remote(quarter, buf2.at[z], s2.at[d - 1], r2.at[d - 1], (peer, r))
        cp.start()
        second.append(cp)
    buf2[z] = total
    for cp in second:
        cp.wait()
    total = buf2[0]
    for d in range(1, rows):
        total = total + buf2[d]
    gram[r] = total
    third = []
    for d in range(1, reach):
        peer = lax.rem(r + d, reach)
        cp = remote(gram.at[r], gram.at[r], s3.at[d - 1], r3.at[d - 1], (z, peer))
        cp.start()
        third.append(cp)
    for cp in third:
        cp.wait()


def image_and_gram(
    rows,
    reach,
    basis,
    near_cols,
    near_count,
    near_blocks,
    marker_rows,
    marker_groups,
    marker_count,
    marker_weights,
    stiffness,
):
    slab, stored = near_cols.shape
    width = basis.shape[1]
    side = BS
    slots = marker_rows.shape[0]
    per = NG // (rows * reach)
    s = lax.axis_index(("row", "reach")).astype(jnp.int32)
    base = s * per
    away = lax.rem(base + NG // 2, NG)
    live = jnp.arange(stored, dtype=jnp.int32)[None, :] < near_count[:, None]
    cols = jnp.where(live, near_cols, reach * slab).reshape(-1)
    mlive = jnp.arange(slots, dtype=jnp.int32) < marker_count[0]
    code = jnp.where(
        marker_groups == base, 0, jnp.where(marker_groups == away, 1, 2)
    ).astype(jnp.int32)
    code = jnp.where(mlive, code, 3)
    blocks = (
        near_blocks.reshape(slab, stored, side, side)
        .transpose(0, 2, 1, 3)
        .reshape(slab, side, stored * side)
    )
    weights = marker_weights.reshape(slots, side, side)
    st = stiffness.reshape(NG, side)
    stiff = jnp.stack(
        [lax.dynamic_index_in_dim(st, g, 0, keepdims=False) for g in (base, away, base + 1)]
    )[:, :, None]
    q = width // reach
    f32, bf16 = jnp.float32, jnp.bfloat16
    dma = pltpu.SemaphoreType.DMA
    image, gram = pl.pallas_call(
        functools.partial(image_kernel, rows, reach),
        out_shape=(
            jax.ShapeDtypeStruct((slab * side, width), f32),
            jax.ShapeDtypeStruct((reach, q, width), f32),
        ),
        in_specs=[SM, SM, SM, VM, VM, VM, VM],
        out_specs=(VM, VM),
        scratch_shapes=[
            pltpu.VMEM((reach * slab + 1, side, width), bf16),
            pltpu.VMEM((3, side, width), f32),
            pltpu.VMEM((2, side, width), f32),
            pltpu.VMEM((3, side, width), bf16),
            pltpu.VMEM((slots, side, width), f32),
            pltpu.VMEM((reach, q, width), f32),
            pltpu.VMEM((reach - 1, q, width), f32),
            pltpu.VMEM((q, width), f32),
            pltpu.VMEM((rows, q, width), f32),
            dma,
            dma,
            dma,
            dma((CHUNKS,)),
            dma((CHUNKS,)),
            dma((CHUNKS,)),
            dma((CHUNKS,)),
            dma,
            dma,
            dma((reach - 1,)),
            dma((reach - 1,)),
            dma((rows - 1,)),
            dma((rows - 1,)),
            dma((reach - 1,)),
            dma((reach - 1,)),
        ],
        compiler_params=pltpu.CompilerParams(
            collective_id=0, has_side_effects=True, vmem_limit_bytes=40 * 1024 * 1024
        ),
    )(
        cols,
        marker_rows,
        code,
        basis.reshape(slab, side, width),
        blocks,
        weights,
        stiff,
    )
    return image, gram.reshape(width, width)


def factor_kernel(root, image, gram, qf, rf, work, full):
    n = gram.shape[0]
    row = lax.broadcasted_iota(jnp.int32, (n, n), 0)
    col = lax.broadcasted_iota(jnp.int32, (n, n), 1)
    work[:, :n] = gram[...]
    work[:, n:] = jnp.where(row == col, 1.0, 0.0)
    sub = lax.broadcasted_iota(jnp.int32, (8, n), 0)
    for p in range(0, n, 8):
        left = work[p : p + 8, :n]
        right = work[p : p + 8, n:]
        cs = [jnp.broadcast_to(left[:, p + j : p + j + 1], (8, n)) for j in range(8)]
        scale = jnp.zeros((8, n), jnp.float32)
        for j in range(8):
            piv = cs[j][j : j + 1, :]
            rs = lax.rsqrt(piv)
            rs = rs * (1.5 - 0.5 * piv * rs * rs)
            scale = jnp.where(sub == j, rs, scale)
            if j == 7:
                break
            mult = jnp.where(sub > j, cs[j] * (rs * rs), 0.0)
            for i in range(j + 1, 8):
                cs[i] = cs[i] - mult * cs[i][j : j + 1, :]
            left = left - mult * left[j : j + 1, :]
            right = right - mult * right[j : j + 1, :]
        left = left * scale
        right = right * scale
        full[p : p + 8, :n] = left
        full[p : p + 8, n:] = right
        if p + 8 < n:
            both = jnp.concatenate([left, right], axis=1)
            change = dot(left, both, 0, 0, HP)
            work[p + 8 :, :] = work[p + 8 :, :] - change[p + 8 :, :]
    rf[...] = jnp.where(col >= row, full[:, :n], 0.0) * (1.0 / root)
    inverse = full[:, n:] * root

    def step(i, carry):
        at = pl.ds(pl.multiple_of(i * 256, 256), 256)
        qf[at] = dot(image[at], inverse, 1, 1, HP)
        return carry

    lax.fori_loop(0, image.shape[0] // 256, step, 0)


def factor(image, gram, total_rows):
    n = gram.shape[0]
    f32 = jnp.float32
    return pl.pallas_call(
        functools.partial(factor_kernel, float(total_rows) ** 0.5),
        out_shape=(
            jax.ShapeDtypeStruct(image.shape, f32),
            jax.ShapeDtypeStruct((n, n), f32),
        ),
        in_specs=[VM, VM],
        out_specs=(VM, VM),
        scratch_shapes=[pltpu.VMEM((n, 2 * n), f32), pltpu.VMEM((n, 2 * n), f32)],
        compiler_params=pltpu.CompilerParams(vmem_limit_bytes=40 * 1024 * 1024),
    )(image, gram)


def pick(index, table):
    count = table.shape[0]
    hot = index[:, None] == jnp.arange(count, dtype=jnp.int32)[None, :]
    taken = jnp.dot(hot.astype(table.dtype), table.reshape(count, -1))
    return taken.reshape((index.shape[0],) + table.shape[1:])


def plain_image_and_gram(
    basis,
    near_cols,
    near_count,
    near_blocks,
    marker_rows,
    marker_groups,
    marker_count,
    marker_weights,
    stiffness,
):
    slab, stored = near_cols.shape
    width = basis.shape[1]
    side = BS
    slots = marker_rows.shape[0]
    groups = NG
    own = basis.reshape(slab, side, width)
    weights = marker_weights.reshape(slots, side, side)
    mlive = jnp.arange(slots, dtype=jnp.int32) < marker_count[0]
    picked = pick(marker_rows, own)
    partial_value = jnp.einsum("mcj,mcd->mjd", weights, picked, preferred_element_type=jnp.float32)
    onehot = (marker_groups[None, :] == jnp.arange(groups, dtype=jnp.int32)[:, None]) & mlive[
        None, :
    ]
    sums = jnp.dot(
        onehot.astype(jnp.float32), partial_value.reshape(slots, side * width), precision=HP
    ).reshape(groups * side, width)
    sums = lax.psum(sums, ("row", "reach"))
    scale = lax.rsqrt(1.0 + jnp.mean(sums * sums, axis=1, keepdims=True))
    force = (stiffness[:, None] * sums * scale).astype(jnp.bfloat16)
    force_rows = jnp.dot(
        onehot.T.astype(jnp.bfloat16),
        force.reshape(groups, side * width),
        preferred_element_type=jnp.float32,
    )
    group_basis = lax.all_gather(basis, "reach", axis=0, tiled=True).reshape(-1, side, width)
    live = jnp.arange(stored, dtype=jnp.int32)[None, :] < near_count[:, None]
    fetched = pick(jnp.where(live, near_cols, -1).reshape(-1), group_basis)
    fetched = fetched.reshape(slab, stored, side, width)
    blocks = near_blocks.reshape(slab, stored, side, side)
    near = jnp.einsum("bkrc,bkcd->brd", blocks, fetched, preferred_element_type=jnp.float32)
    force_rows = force_rows.astype(jnp.bfloat16).reshape(slots, side, width)
    contrib = jnp.einsum("mcj,mjd->mcd", weights, force_rows, preferred_element_type=jnp.float32)
    rowhot = (
        (marker_rows[None, :] == jnp.arange(slab, dtype=jnp.int32)[:, None]) & mlive[None, :]
    ).astype(jnp.float32)
    spread = jnp.dot(rowhot, contrib.reshape(slots, side * width), precision=HP).reshape(
        slab, side, width
    )
    image = (near + spread).reshape(slab * side, width)
    gram = lax.psum(jnp.dot(image.T, image, precision=HP), ("row", "reach"))
    return image, gram


def solution(mesh):
    rows, reach = mesh.shape["row"], mesh.shape["reach"]
    devices = rows * reach
    paired = reach == 4 and rows % 2 == 0 and NG % devices == 0 and NG // devices >= 2

    def local(*args):
        if paired:
            image, gram = image_and_gram(rows, reach, *args)
        else:
            image, gram = plain_image_and_gram(*args)
        return factor(image, gram, image.shape[0] * devices)

    return jax.shard_map(
        local,
        mesh=mesh,
        in_specs=(
            P(("row", "reach"), None),
            P(("row", "reach"), None),
            P(("row", "reach")),
            P(("row", "reach"), None, None),
            P(("row", "reach")),
            P(("row", "reach")),
            P(("row", "reach")),
            P(("row", "reach"), None),
            P(),
        ),
        out_specs=(P(("row", "reach"), None), P()),
        check_vma=False,
    )
```

```python
import functools

import jax
import jax.numpy as jnp
from jax import lax
from jax.experimental import pallas as pl
from jax.experimental.pallas import tpu as pltpu
from jax.sharding import PartitionSpec as P

BS = 64
NG = 64
CHUNKS = 4
HP = lax.Precision.HIGHEST
MESH = pl.DeviceIdType.MESH
VM = pl.BlockSpec(memory_space=pltpu.VMEM)
SM = pl.BlockSpec(memory_space=pltpu.SMEM)


def dot(a, b, da, db, precision=None):
    return lax.dot_general(
        a, b, (((da,), (db,)), ((), ())), precision=precision, preferred_element_type=jnp.float32
    )


def image_kernel(
    rows,
    reach,
    cols,
    mrow,
    code,
    basis,
    blocks,
    weights,
    stiff,
    image,
    gram,
    grp,
    sums,
    other,
    force,
    contrib,
    part,
    buf1,
    quarter,
    buf2,
    local_sem,
    sib_send,
    sib_recv,
    y_send,
    y_recv,
    f_send,
    f_recv,
    m_send,
    m_recv,
    s1,
    r1,
    s2,
    r2,
    s3,
    r3,
):
    z = lax.axis_index("row")
    r = lax.axis_index("reach")
    slab, side, width = basis.shape
    stored = blocks.shape[1]
    slots = weights.shape[0]
    core = lax.rem(r, 2)
    sib = r + 1 - 2 * core
    far = lax.rem(r + 2, reach)

    barrier = pltpu.get_barrier_semaphore()
    for d in range(1, reach):
        pl.semaphore_signal(
            barrier, inc=1, device_id=(z, lax.rem(r + d, reach)), device_id_type=MESH
        )
    for d in range(1, rows):
        pl.semaphore_signal(
            barrier, inc=1, device_id=(lax.rem(z + d, rows), r), device_id_type=MESH
        )
    pl.semaphore_wait(barrier, reach + rows - 2)

    def remote(src, dst, ss, rs, dev):
        return pltpu.make_async_remote_copy(
            src_ref=src, dst_ref=dst, send_sem=ss, recv_sem=rs, device_id=dev, device_id_type=MESH
        )

    step = slab // CHUNKS
    to_far = []
    for c in range(CHUNKS):
        cp = remote(
            basis.at[pl.ds(c * step, step)],
            grp.at[pl.ds(r * slab + c * step, step)],
            y_send.at[c],
            y_recv.at[c],
            (z, far),
        )
        cp.start()
        to_far.append(cp)
    to_sib = remote(basis, grp.at[pl.ds(r * slab, slab)], sib_send, sib_recv, (z, sib))
    to_sib.start()
    own = pltpu.make_async_copy(basis, grp.at[pl.ds(r * slab, slab)], local_sem)
    own.start()
    grp[reach * slab] = jnp.zeros((side, width), grp.dtype)

    sums[...] = jnp.zeros_like(sums)

    def gather_step(m, carry):
        value = dot(weights[m], basis[mrow[m]], 0, 0)
        for g in range(3):
            sums[g] = sums[g] + jnp.where(code[m] == g, 1.0, 0.0) * value
        return carry

    lax.fori_loop(0, slots, gather_step, 0)
    swap = remote(
        sums.at[pl.ds(0, 2)], other, m_send, m_recv, (lax.rem(z + rows // 2, rows), r)
    )
    swap.start()

    def force_of(total, g):
        scale = lax.rsqrt(1.0 + jnp.mean(total * total, axis=1, keepdims=True))
        return (stiff[g] * total * scale).astype(jnp.bfloat16)

    force[2] = force_of(sums[2], 2)
    fwd = []
    for c in range(CHUNKS):
        to_far[c].wait_recv()
        place = pl.ds(far * slab + c * step, step)
        cp = remote(grp.at[place], grp.at[place], f_send.at[c], f_recv.at[c], (z, sib))
        cp.start()
        fwd.append(cp)
    swap.wait()
    force[0] = force_of(sums[0] + other[1], 0)
    force[1] = force_of(sums[1] + other[0], 1)

    def spread_step(m, carry):
        contrib[m] = dot(weights[m], force[jnp.minimum(code[m], 2)], 1, 0)
        return carry

    lax.fori_loop(0, slots, spread_step, 0)

    own.wait()
    to_sib.wait()
    for c in range(CHUNKS):
        to_far[c].wait_send()
        fwd[c].wait()

    def near_step(i, carry):
        acc = dot(blocks[i, 0], grp[cols[i * stored]], 1, 0)
        for k in range(1, stored):
            acc = acc + dot(blocks[i, k], grp[cols[i * stored + k]], 1, 0)
        for m in range(slots):
            hit = jnp.where((mrow[m] == i) & (code[m] < 3), 1.0, 0.0)
            acc = acc + hit * contrib[m]
        image[pl.ds(pl.multiple_of(i * side, side), side)] = acc
        return carry

    lax.fori_loop(0, slab, near_step, 0)

    part[...] = jnp.zeros_like(part)

    def gram_step(i, carry):
        x = image[pl.ds(pl.multiple_of(i * 256, 256), 256)]
        part[...] += dot(x, x, 0, 0, HP).reshape(part.shape)
        return carry

    lax.fori_loop(0, slab * side // 256, gram_step, 0)

    first = []
    for d in range(1, reach):
        peer = lax.rem(r + d, reach)
        cp = remote(part.at[peer], buf1.at[d - 1], s1.at[d - 1], r1.at[d - 1], (z, peer))
        cp.start()
        first.append(cp)
    for cp in first:
        cp.wait()
    total = part[r]
    for d in range(reach - 1):
        total = total + buf1[d]
    quarter[...] = total
    second = []
    for d in range(1, rows):
        peer = lax.rem(z + d, rows)
        cp = remote(quarter, buf2.at[z], s2.at[d - 1], r2.at[d - 1], (peer, r))
        cp.start()
        second.append(cp)
    buf2[z] = total
    for cp in second:
        cp.wait()
    total = buf2[0]
    for d in range(1, rows):
        total = total + buf2[d]
    gram[r] = total
    third = []
    for d in range(1, reach):
        peer = lax.rem(r + d, reach)
        cp = remote(gram.at[r], gram.at[r], s3.at[d - 1], r3.at[d - 1], (z, peer))
        cp.start()
        third.append(cp)
    for cp in third:
        cp.wait()


def image_and_gram(
    rows,
    reach,
    basis,
    near_cols,
    near_count,
    near_blocks,
    marker_rows,
    marker_groups,
    marker_count,
    marker_weights,
    stiffness,
):
    slab, stored = near_cols.shape
    width = basis.shape[1]
    side = BS
    slots = marker_rows.shape[0]
    per = NG // (rows * reach)
    s = lax.axis_index(("row", "reach")).astype(jnp.int32)
    base = s * per
    away = lax.rem(base + NG // 2, NG)
    live = jnp.arange(stored, dtype=jnp.int32)[None, :] < near_count[:, None]
    cols = jnp.where(live, near_cols, reach * slab).reshape(-1)
    mlive = jnp.arange(slots, dtype=jnp.int32) < marker_count[0]
    code = jnp.where(
        marker_groups == base, 0, jnp.where(marker_groups == away, 1, 2)
    ).astype(jnp.int32)
    code = jnp.where(mlive, code, 3)
    blocks = near_blocks.reshape(slab, stored, side, side)
    weights = marker_weights.reshape(slots, side, side)
    st = stiffness.reshape(NG, side)
    stiff = jnp.stack(
        [lax.dynamic_index_in_dim(st, g, 0, keepdims=False) for g in (base, away, base + 1)]
    )[:, :, None]
    q = width // reach
    f32, bf16 = jnp.float32, jnp.bfloat16
    dma = pltpu.SemaphoreType.DMA
    image, gram = pl.pallas_call(
        functools.partial(image_kernel, rows, reach),
        out_shape=(
            jax.ShapeDtypeStruct((slab * side, width), f32),
            jax.ShapeDtypeStruct((reach, q, width), f32),
        ),
        in_specs=[SM, SM, SM, VM, VM, VM, VM],
        out_specs=(VM, VM),
        scratch_shapes=[
            pltpu.VMEM((reach * slab + 1, side, width), bf16),
            pltpu.VMEM((3, side, width), f32),
            pltpu.VMEM((2, side, width), f32),
            pltpu.VMEM((3, side, width), bf16),
            pltpu.VMEM((slots, side, width), f32),
            pltpu.VMEM((reach, q, width), f32),
            pltpu.VMEM((reach - 1, q, width), f32),
            pltpu.VMEM((q, width), f32),
            pltpu.VMEM((rows, q, width), f32),
            dma,
            dma,
            dma,
            dma((CHUNKS,)),
            dma((CHUNKS,)),
            dma((CHUNKS,)),
            dma((CHUNKS,)),
            dma,
            dma,
            dma((reach - 1,)),
            dma((reach - 1,)),
            dma((rows - 1,)),
            dma((rows - 1,)),
            dma((reach - 1,)),
            dma((reach - 1,)),
        ],
        compiler_params=pltpu.CompilerParams(
            collective_id=0, has_side_effects=True, vmem_limit_bytes=40 * 1024 * 1024
        ),
    )(
        cols,
        marker_rows,
        code,
        basis.reshape(slab, side, width),
        blocks,
        weights,
        stiff,
    )
    return image, gram.reshape(width, width)


def factor_kernel(root, image, gram, qf, rf, work, full):
    n = gram.shape[0]
    row = lax.broadcasted_iota(jnp.int32, (n, n), 0)
    col = lax.broadcasted_iota(jnp.int32, (n, n), 1)
    work[:, :n] = gram[...]
    work[:, n:] = jnp.where(row == col, 1.0, 0.0)
    sub = lax.broadcasted_iota(jnp.int32, (8, n), 0)
    for p in range(0, n, 8):
        left = work[p : p + 8, :n]
        right = work[p : p + 8, n:]
        cs = [jnp.broadcast_to(left[:, p + j : p + j + 1], (8, n)) for j in range(8)]
        scale = jnp.zeros((8, n), jnp.float32)
        for j in range(8):
            piv = cs[j][j : j + 1, :]
            rs = lax.rsqrt(piv)
            rs = rs * (1.5 - 0.5 * piv * rs * rs)
            scale = jnp.where(sub == j, rs, scale)
            if j == 7:
                break
            mult = jnp.where(sub > j, cs[j] * (rs * rs), 0.0)
            for i in range(j + 1, 8):
                cs[i] = cs[i] - mult * cs[i][j : j + 1, :]
            left = left - mult * left[j : j + 1, :]
            right = right - mult * right[j : j + 1, :]
        left = left * scale
        right = right * scale
        full[p : p + 8, :n] = left
        full[p : p + 8, n:] = right
        if p + 8 < n:
            both = jnp.concatenate([left, right], axis=1)
            change = dot(left, both, 0, 0, HP)
            work[p + 8 :, :] = work[p + 8 :, :] - change[p + 8 :, :]
    rf[...] = jnp.where(col >= row, full[:, :n], 0.0) * (1.0 / root)
    inverse = full[:, n:] * root

    def step(i, carry):
        at = pl.ds(pl.multiple_of(i * 256, 256), 256)
        qf[at] = dot(image[at], inverse, 1, 1, HP)
        return carry

    lax.fori_loop(0, image.shape[0] // 256, step, 0)


def factor(image, gram, total_rows):
    n = gram.shape[0]
    f32 = jnp.float32
    return pl.pallas_call(
        functools.partial(factor_kernel, float(total_rows) ** 0.5),
        out_shape=(
            jax.ShapeDtypeStruct(image.shape, f32),
            jax.ShapeDtypeStruct((n, n), f32),
        ),
        in_specs=[VM, VM],
        out_specs=(VM, VM),
        scratch_shapes=[pltpu.VMEM((n, 2 * n), f32), pltpu.VMEM((n, 2 * n), f32)],
        compiler_params=pltpu.CompilerParams(vmem_limit_bytes=40 * 1024 * 1024),
    )(image, gram)


def pick(index, table):
    count = table.shape[0]
    hot = index[:, None] == jnp.arange(count, dtype=jnp.int32)[None, :]
    taken = jnp.dot(hot.astype(table.dtype), table.reshape(count, -1))
    return taken.reshape((index.shape[0],) + table.shape[1:])


def plain_image_and_gram(
    basis,
    near_cols,
    near_count,
    near_blocks,
    marker_rows,
    marker_groups,
    marker_count,
    marker_weights,
    stiffness,
):
    slab, stored = near_cols.shape
    width = basis.shape[1]
    side = BS
    slots = marker_rows.shape[0]
    groups = NG
    own = basis.reshape(slab, side, width)
    weights = marker_weights.reshape(slots, side, side)
    mlive = jnp.arange(slots, dtype=jnp.int32) < marker_count[0]
    picked = pick(marker_rows, own)
    partial_value = jnp.einsum("mcj,mcd->mjd", weights, picked, preferred_element_type=jnp.float32)
    onehot = (marker_groups[None, :] == jnp.arange(groups, dtype=jnp.int32)[:, None]) & mlive[
        None, :
    ]
    sums = jnp.dot(
        onehot.astype(jnp.float32), partial_value.reshape(slots, side * width), precision=HP
    ).reshape(groups * side, width)
    sums = lax.psum(sums, ("row", "reach"))
    scale = lax.rsqrt(1.0 + jnp.mean(sums * sums, axis=1, keepdims=True))
    force = (stiffness[:, None] * sums * scale).astype(jnp.bfloat16)
    force_rows = jnp.dot(
        onehot.T.astype(jnp.bfloat16),
        force.reshape(groups, side * width),
        preferred_element_type=jnp.float32,
    )
    group_basis = lax.all_gather(basis, "reach", axis=0, tiled=True).reshape(-1, side, width)
    live = jnp.arange(stored, dtype=jnp.int32)[None, :] < near_count[:, None]
    fetched = pick(jnp.where(live, near_cols, -1).reshape(-1), group_basis)
    fetched = fetched.reshape(slab, stored, side, width)
    blocks = near_blocks.reshape(slab, stored, side, side)
    near = jnp.einsum("bkrc,bkcd->brd", blocks, fetched, preferred_element_type=jnp.float32)
    force_rows = force_rows.astype(jnp.bfloat16).reshape(slots, side, width)
    contrib = jnp.einsum("mcj,mjd->mcd", weights, force_rows, preferred_element_type=jnp.float32)
    rowhot = (
        (marker_rows[None, :] == jnp.arange(slab, dtype=jnp.int32)[:, None]) & mlive[None, :]
    ).astype(jnp.float32)
    spread = jnp.dot(rowhot, contrib.reshape(slots, side * width), precision=HP).reshape(
        slab, side, width
    )
    image = (near + spread).reshape(slab * side, width)
    gram = lax.psum(jnp.dot(image.T, image, precision=HP), ("row", "reach"))
    return image, gram


def solution(mesh):
    rows, reach = mesh.shape["row"], mesh.shape["reach"]
    devices = rows * reach
    paired = reach == 4 and rows % 2 == 0 and NG % devices == 0 and NG // devices >= 2

    def local(*args):
        if paired:
            image, gram = image_and_gram(rows, reach, *args)
        else:
            image, gram = plain_image_and_gram(*args)
        return factor(image, gram, image.shape[0] * devices)

    return jax.shard_map(
        local,
        mesh=mesh,
        in_specs=(
            P(("row", "reach"), None),
            P(("row", "reach"), None),
            P(("row", "reach")),
            P(("row", "reach"), None, None),
            P(("row", "reach")),
            P(("row", "reach")),
            P(("row", "reach")),
            P(("row", "reach"), None),
            P(),
        ),
        out_specs=(P(("row", "reach"), None), P()),
        check_vma=False,
    )
```

```python
import functools

import jax
import jax.numpy as jnp
from jax import lax
from jax.experimental import pallas as pl
from jax.experimental.pallas import tpu as pltpu
from jax.sharding import PartitionSpec as P

BS = 64
NG = 64
CHUNKS = 4
HP = lax.Precision.HIGHEST
MESH = pl.DeviceIdType.MESH
VM = pl.BlockSpec(memory_space=pltpu.VMEM)
SM = pl.BlockSpec(memory_space=pltpu.SMEM)


def dot(a, b, da, db, precision=None):
    return lax.dot_general(
        a, b, (((da,), (db,)), ((), ())), precision=precision, preferred_element_type=jnp.float32
    )


def image_kernel(
    rows,
    reach,
    cols,
    mrow,
    code,
    basis,
    blocks,
    weights,
    stiff,
    image,
    gram,
    grp,
    sums,
    other,
    force,
    contrib,
    part,
    buf1,
    quarter,
    buf2,
    local_sem,
    sib_send,
    sib_recv,
    y_send,
    y_recv,
    f_send,
    f_recv,
    m_send,
    m_recv,
    s1,
    r1,
    s2,
    r2,
    s3,
    r3,
):
    z = lax.axis_index("row")
    r = lax.axis_index("reach")
    slab, side, width = basis.shape
    stored = blocks.shape[1]
    slots = weights.shape[0]
    core = lax.rem(r, 2)
    sib = r + 1 - 2 * core
    far = lax.rem(r + 2, reach)

    barrier = pltpu.get_barrier_semaphore()
    for d in range(1, reach):
        pl.semaphore_signal(
            barrier, inc=1, device_id=(z, lax.rem(r + d, reach)), device_id_type=MESH
        )
    for d in range(1, rows):
        pl.semaphore_signal(
            barrier, inc=1, device_id=(lax.rem(z + d, rows), r), device_id_type=MESH
        )
    pl.semaphore_wait(barrier, reach + rows - 2)

    def remote(src, dst, ss, rs, dev):
        return pltpu.make_async_remote_copy(
            src_ref=src, dst_ref=dst, send_sem=ss, recv_sem=rs, device_id=dev, device_id_type=MESH
        )

    step = slab // CHUNKS
    to_far = []
    for c in range(CHUNKS):
        cp = remote(
            basis.at[pl.ds(c * step, step)],
            grp.at[pl.ds(r * slab + c * step, step)],
            y_send.at[c],
            y_recv.at[c],
            (z, far),
        )
        cp.start()
        to_far.append(cp)
    to_sib = remote(basis, grp.at[pl.ds(r * slab, slab)], sib_send, sib_recv, (z, sib))
    to_sib.start()
    own = pltpu.make_async_copy(basis, grp.at[pl.ds(r * slab, slab)], local_sem)
    own.start()
    grp[reach * slab] = jnp.zeros((side, width), grp.dtype)

    sums[...] = jnp.zeros_like(sums)

    def gather_step(m, carry):
        value = dot(weights[m], basis[mrow[m]], 0, 0)
        for g in range(3):
            sums[g] = sums[g] + jnp.where(code[m] == g, 1.0, 0.0) * value
        return carry

    lax.fori_loop(0, slots, gather_step, 0)
    swap = remote(
        sums.at[pl.ds(0, 2)], other, m_send, m_recv, (lax.rem(z + rows // 2, rows), r)
    )
    swap.start()

    def force_of(total, g):
        scale = lax.rsqrt(1.0 + jnp.mean(total * total, axis=1, keepdims=True))
        return (stiff[g] * total * scale).astype(jnp.bfloat16)

    force[2] = force_of(sums[2], 2)
    fwd = []
    for c in range(CHUNKS):
        to_far[c].wait_recv()
        place = pl.ds(far * slab + c * step, step)
        cp = remote(grp.at[place], grp.at[place], f_send.at[c], f_recv.at[c], (z, sib))
        cp.start()
        fwd.append(cp)
    swap.wait()
    force[0] = force_of(sums[0] + other[1], 0)
    force[1] = force_of(sums[1] + other[0], 1)

    def spread_step(m, carry):
        contrib[m] = dot(weights[m], force[jnp.minimum(code[m], 2)], 1, 0)
        return carry

    lax.fori_loop(0, slots, spread_step, 0)

    def own_step(i, carry):
        acc = dot(blocks[i, 0], basis[i], 1, 0)
        for m in range(slots):
            hit = jnp.where((mrow[m] == i) & (code[m] < 3), 1.0, 0.0)
            acc = acc + hit * contrib[m]
        image[pl.ds(pl.multiple_of(i * side, side), side)] = acc
        return carry

    lax.fori_loop(0, slab, own_step, 0)

    own.wait()
    to_sib.wait()
    for c in range(CHUNKS):
        to_far[c].wait_send()
        fwd[c].wait()

    def near_step(i, carry):
        at = pl.ds(pl.multiple_of(i * side, side), side)
        acc = image[at]
        for k in range(1, stored):
            acc = acc + dot(blocks[i, k], grp[cols[i * stored + k]], 1, 0)
        image[at] = acc
        return carry

    lax.fori_loop(0, slab, near_step, 0)

    part[...] = jnp.zeros_like(part)

    def gram_step(i, carry):
        x = image[pl.ds(pl.multiple_of(i * 256, 256), 256)]
        part[...] += dot(x, x, 0, 0, HP).reshape(part.shape)
        return carry

    lax.fori_loop(0, slab * side // 256, gram_step, 0)

    first = []
    for d in range(1, reach):
        peer = lax.rem(r + d, reach)
        cp = remote(part.at[peer], buf1.at[d - 1], s1.at[d - 1], r1.at[d - 1], (z, peer))
        cp.start()
        first.append(cp)
    for cp in first:
        cp.wait()
    total = part[r]
    for d in range(reach - 1):
        total = total + buf1[d]
    quarter[...] = total
    second = []
    for d in range(1, rows):
        peer = lax.rem(z + d, rows)
        cp = remote(quarter, buf2.at[z], s2.at[d - 1], r2.at[d - 1], (peer, r))
        cp.start()
        second.append(cp)
    buf2[z] = total
    for cp in second:
        cp.wait()
    total = buf2[0]
    for d in range(1, rows):
        total = total + buf2[d]
    gram[r] = total
    third = []
    for d in range(1, reach):
        peer = lax.rem(r + d, reach)
        cp = remote(gram.at[r], gram.at[r], s3.at[d - 1], r3.at[d - 1], (z, peer))
        cp.start()
        third.append(cp)
    for cp in third:
        cp.wait()


def image_and_gram(
    rows,
    reach,
    basis,
    near_cols,
    near_count,
    near_blocks,
    marker_rows,
    marker_groups,
    marker_count,
    marker_weights,
    stiffness,
):
    slab, stored = near_cols.shape
    width = basis.shape[1]
    side = BS
    slots = marker_rows.shape[0]
    per = NG // (rows * reach)
    s = lax.axis_index(("row", "reach")).astype(jnp.int32)
    base = s * per
    away = lax.rem(base + NG // 2, NG)
    live = jnp.arange(stored, dtype=jnp.int32)[None, :] < near_count[:, None]
    cols = jnp.where(live, near_cols, reach * slab).reshape(-1)
    mlive = jnp.arange(slots, dtype=jnp.int32) < marker_count[0]
    code = jnp.where(
        marker_groups == base, 0, jnp.where(marker_groups == away, 1, 2)
    ).astype(jnp.int32)
    code = jnp.where(mlive, code, 3)
    blocks = near_blocks.reshape(slab, stored, side, side)
    weights = marker_weights.reshape(slots, side, side)
    st = stiffness.reshape(NG, side)
    stiff = jnp.stack(
        [lax.dynamic_index_in_dim(st, g, 0, keepdims=False) for g in (base, away, base + 1)]
    )[:, :, None]
    q = width // reach
    f32, bf16 = jnp.float32, jnp.bfloat16
    dma = pltpu.SemaphoreType.DMA
    image, gram = pl.pallas_call(
        functools.partial(image_kernel, rows, reach),
        out_shape=(
            jax.ShapeDtypeStruct((slab * side, width), f32),
            jax.ShapeDtypeStruct((reach, q, width), f32),
        ),
        in_specs=[SM, SM, SM, VM, VM, VM, VM],
        out_specs=(VM, VM),
        scratch_shapes=[
            pltpu.VMEM((reach * slab + 1, side, width), bf16),
            pltpu.VMEM((3, side, width), f32),
            pltpu.VMEM((2, side, width), f32),
            pltpu.VMEM((3, side, width), bf16),
            pltpu.VMEM((slots, side, width), f32),
            pltpu.VMEM((reach, q, width), f32),
            pltpu.VMEM((reach - 1, q, width), f32),
            pltpu.VMEM((q, width), f32),
            pltpu.VMEM((rows, q, width), f32),
            dma,
            dma,
            dma,
            dma((CHUNKS,)),
            dma((CHUNKS,)),
            dma((CHUNKS,)),
            dma((CHUNKS,)),
            dma,
            dma,
            dma((reach - 1,)),
            dma((reach - 1,)),
            dma((rows - 1,)),
            dma((rows - 1,)),
            dma((reach - 1,)),
            dma((reach - 1,)),
        ],
        compiler_params=pltpu.CompilerParams(
            collective_id=0, has_side_effects=True, vmem_limit_bytes=40 * 1024 * 1024
        ),
    )(
        cols,
        marker_rows,
        code,
        basis.reshape(slab, side, width),
        blocks,
        weights,
        stiff,
    )
    return image, gram.reshape(width, width)


def factor_kernel(root, image, gram, qf, rf, work, full):
    n = gram.shape[0]
    row = lax.broadcasted_iota(jnp.int32, (n, n), 0)
    col = lax.broadcasted_iota(jnp.int32, (n, n), 1)
    work[:, :n] = gram[...]
    work[:, n:] = jnp.where(row == col, 1.0, 0.0)
    sub = lax.broadcasted_iota(jnp.int32, (8, n), 0)
    for p in range(0, n, 8):
        left = work[p : p + 8, :n]
        right = work[p : p + 8, n:]
        cs = [jnp.broadcast_to(left[:, p + j : p + j + 1], (8, n)) for j in range(8)]
        scale = jnp.zeros((8, n), jnp.float32)
        for j in range(8):
            piv = cs[j][j : j + 1, :]
            rs = lax.rsqrt(piv)
            rs = rs * (1.5 - 0.5 * piv * rs * rs)
            scale = jnp.where(sub == j, rs, scale)
            if j == 7:
                break
            mult = jnp.where(sub > j, cs[j] * (rs * rs), 0.0)
            for i in range(j + 1, 8):
                cs[i] = cs[i] - mult * cs[i][j : j + 1, :]
            left = left - mult * left[j : j + 1, :]
            right = right - mult * right[j : j + 1, :]
        left = left * scale
        right = right * scale
        full[p : p + 8, :n] = left
        full[p : p + 8, n:] = right
        if p + 8 < n:
            both = jnp.concatenate([left, right], axis=1)
            change = dot(left, both, 0, 0, HP)
            work[p + 8 :, :] = work[p + 8 :, :] - change[p + 8 :, :]
    rf[...] = jnp.where(col >= row, full[:, :n], 0.0) * (1.0 / root)
    inverse = full[:, n:] * root

    def step(i, carry):
        at = pl.ds(pl.multiple_of(i * 256, 256), 256)
        qf[at] = dot(image[at], inverse, 1, 1, HP)
        return carry

    lax.fori_loop(0, image.shape[0] // 256, step, 0)


def factor(image, gram, total_rows):
    n = gram.shape[0]
    f32 = jnp.float32
    return pl.pallas_call(
        functools.partial(factor_kernel, float(total_rows) ** 0.5),
        out_shape=(
            jax.ShapeDtypeStruct(image.shape, f32),
            jax.ShapeDtypeStruct((n, n), f32),
        ),
        in_specs=[VM, VM],
        out_specs=(VM, VM),
        scratch_shapes=[pltpu.VMEM((n, 2 * n), f32), pltpu.VMEM((n, 2 * n), f32)],
        compiler_params=pltpu.CompilerParams(vmem_limit_bytes=40 * 1024 * 1024),
    )(image, gram)


def pick(index, table):
    count = table.shape[0]
    hot = index[:, None] == jnp.arange(count, dtype=jnp.int32)[None, :]
    taken = jnp.dot(hot.astype(table.dtype), table.reshape(count, -1))
    return taken.reshape((index.shape[0],) + table.shape[1:])


def plain_image_and_gram(
    basis,
    near_cols,
    near_count,
    near_blocks,
    marker_rows,
    marker_groups,
    marker_count,
    marker_weights,
    stiffness,
):
    slab, stored = near_cols.shape
    width = basis.shape[1]
    side = BS
    slots = marker_rows.shape[0]
    groups = NG
    own = basis.reshape(slab, side, width)
    weights = marker_weights.reshape(slots, side, side)
    mlive = jnp.arange(slots, dtype=jnp.int32) < marker_count[0]
    picked = pick(marker_rows, own)
    partial_value = jnp.einsum("mcj,mcd->mjd", weights, picked, preferred_element_type=jnp.float32)
    onehot = (marker_groups[None, :] == jnp.arange(groups, dtype=jnp.int32)[:, None]) & mlive[
        None, :
    ]
    sums = jnp.dot(
        onehot.astype(jnp.float32), partial_value.reshape(slots, side * width), precision=HP
    ).reshape(groups * side, width)
    sums = lax.psum(sums, ("row", "reach"))
    scale = lax.rsqrt(1.0 + jnp.mean(sums * sums, axis=1, keepdims=True))
    force = (stiffness[:, None] * sums * scale).astype(jnp.bfloat16)
    force_rows = jnp.dot(
        onehot.T.astype(jnp.bfloat16),
        force.reshape(groups, side * width),
        preferred_element_type=jnp.float32,
    )
    group_basis = lax.all_gather(basis, "reach", axis=0, tiled=True).reshape(-1, side, width)
    live = jnp.arange(stored, dtype=jnp.int32)[None, :] < near_count[:, None]
    fetched = pick(jnp.where(live, near_cols, -1).reshape(-1), group_basis)
    fetched = fetched.reshape(slab, stored, side, width)
    blocks = near_blocks.reshape(slab, stored, side, side)
    near = jnp.einsum("bkrc,bkcd->brd", blocks, fetched, preferred_element_type=jnp.float32)
    force_rows = force_rows.astype(jnp.bfloat16).reshape(slots, side, width)
    contrib = jnp.einsum("mcj,mjd->mcd", weights, force_rows, preferred_element_type=jnp.float32)
    rowhot = (
        (marker_rows[None, :] == jnp.arange(slab, dtype=jnp.int32)[:, None]) & mlive[None, :]
    ).astype(jnp.float32)
    spread = jnp.dot(rowhot, contrib.reshape(slots, side * width), precision=HP).reshape(
        slab, side, width
    )
    image = (near + spread).reshape(slab * side, width)
    gram = lax.psum(jnp.dot(image.T, image, precision=HP), ("row", "reach"))
    return image, gram


def solution(mesh):
    rows, reach = mesh.shape["row"], mesh.shape["reach"]
    devices = rows * reach
    paired = reach == 4 and rows % 2 == 0 and NG % devices == 0 and NG // devices >= 2

    def local(*args):
        if paired:
            image, gram = image_and_gram(rows, reach, *args)
        else:
            image, gram = plain_image_and_gram(*args)
        return factor(image, gram, image.shape[0] * devices)

    return jax.shard_map(
        local,
        mesh=mesh,
        in_specs=(
            P(("row", "reach"), None),
            P(("row", "reach"), None),
            P(("row", "reach")),
            P(("row", "reach"), None, None),
            P(("row", "reach")),
            P(("row", "reach")),
            P(("row", "reach")),
            P(("row", "reach"), None),
            P(),
        ),
        out_specs=(P(("row", "reach"), None), P()),
        check_vma=False,
    )
```

```python
import functools

import jax
import jax.numpy as jnp
from jax import lax
from jax.experimental import pallas as pl
from jax.experimental.pallas import tpu as pltpu
from jax.sharding import PartitionSpec as P

BS = 64
NG = 64
CHUNKS = 4
TOGETHER = 4
HP = lax.Precision.HIGHEST
MESH = pl.DeviceIdType.MESH
VM = pl.BlockSpec(memory_space=pltpu.VMEM)
SM = pl.BlockSpec(memory_space=pltpu.SMEM)


def dot(a, b, da, db, precision=None):
    return lax.dot_general(
        a, b, (((da,), (db,)), ((), ())), precision=precision, preferred_element_type=jnp.float32
    )


def image_kernel(
    rows,
    reach,
    cols,
    mrow,
    code,
    basis,
    blocks,
    weights,
    stiff,
    image,
    gram,
    grp,
    sums,
    other,
    force,
    contrib,
    part,
    buf1,
    quarter,
    buf2,
    local_sem,
    sib_send,
    sib_recv,
    y_send,
    y_recv,
    f_send,
    f_recv,
    m_send,
    m_recv,
    s1,
    r1,
    s2,
    r2,
    s3,
    r3,
):
    z = lax.axis_index("row")
    r = lax.axis_index("reach")
    slab, side, width = basis.shape
    stored = blocks.shape[1]
    slots = weights.shape[0]
    core = lax.rem(r, 2)
    sib = r + 1 - 2 * core
    far = lax.rem(r + 2, reach)

    barrier = pltpu.get_barrier_semaphore()
    for d in range(1, reach):
        pl.semaphore_signal(
            barrier, inc=1, device_id=(z, lax.rem(r + d, reach)), device_id_type=MESH
        )
    for d in range(1, rows):
        pl.semaphore_signal(
            barrier, inc=1, device_id=(lax.rem(z + d, rows), r), device_id_type=MESH
        )
    pl.semaphore_wait(barrier, reach + rows - 2)

    def remote(src, dst, ss, rs, dev):
        return pltpu.make_async_remote_copy(
            src_ref=src, dst_ref=dst, send_sem=ss, recv_sem=rs, device_id=dev, device_id_type=MESH
        )

    step = slab // CHUNKS
    to_far = []
    for c in range(CHUNKS):
        cp = remote(
            basis.at[pl.ds(c * step, step)],
            grp.at[pl.ds(r * slab + c * step, step)],
            y_send.at[c],
            y_recv.at[c],
            (z, far),
        )
        cp.start()
        to_far.append(cp)
    to_sib = remote(basis, grp.at[pl.ds(r * slab, slab)], sib_send, sib_recv, (z, sib))
    to_sib.start()
    own = pltpu.make_async_copy(basis, grp.at[pl.ds(r * slab, slab)], local_sem)
    own.start()
    grp[reach * slab] = jnp.zeros((side, width), grp.dtype)

    sums[...] = jnp.zeros_like(sums)

    def gather_step(t, carry):
        ms = [t * TOGETHER + u for u in range(TOGETHER)]
        values = [dot(weights[m], basis[mrow[m]], 0, 0) for m in ms]
        for g in range(3):
            total = sums[g]
            for m, value in zip(ms, values):
                total = total + jnp.where(code[m] == g, 1.0, 0.0) * value
            sums[g] = total
        return carry

    lax.fori_loop(0, slots // TOGETHER, gather_step, 0)
    swap = remote(
        sums.at[pl.ds(0, 2)], other, m_send, m_recv, (lax.rem(z + rows // 2, rows), r)
    )
    swap.start()

    def force_of(total, g):
        scale = lax.rsqrt(1.0 + jnp.mean(total * total, axis=1, keepdims=True))
        return (stiff[g] * total * scale).astype(jnp.bfloat16)

    force[2] = force_of(sums[2], 2)
    fwd = []
    for c in range(CHUNKS):
        to_far[c].wait_recv()
        place = pl.ds(far * slab + c * step, step)
        cp = remote(grp.at[place], grp.at[place], f_send.at[c], f_recv.at[c], (z, sib))
        cp.start()
        fwd.append(cp)
    swap.wait()
    force[0] = force_of(sums[0] + other[1], 0)
    force[1] = force_of(sums[1] + other[0], 1)

    def spread_step(t, carry):
        ms = [t * TOGETHER + u for u in range(TOGETHER)]
        values = [dot(weights[m], force[jnp.minimum(code[m], 2)], 1, 0) for m in ms]
        for m, value in zip(ms, values):
            contrib[m] = value
        return carry

    lax.fori_loop(0, slots // TOGETHER, spread_step, 0)

    own.wait()
    to_sib.wait()
    for c in range(CHUNKS):
        to_far[c].wait_send()
        fwd[c].wait()

    def near_step(t, carry):
        lines = [t * TOGETHER + u for u in range(TOGETHER)]
        accs = [dot(blocks[i, 0], grp[cols[i * stored]], 1, 0) for i in lines]
        for k in range(1, stored):
            accs = [
                acc + dot(blocks[i, k], grp[cols[i * stored + k]], 1, 0)
                for i, acc in zip(lines, accs)
            ]
        for m in range(slots):
            term = contrib[m]
            accs = [
                acc + jnp.where((mrow[m] == i) & (code[m] < 3), 1.0, 0.0) * term
                for i, acc in zip(lines, accs)
            ]
        for i, acc in zip(lines, accs):
            image[pl.ds(pl.multiple_of(i * side, side), side)] = acc
        return carry

    lax.fori_loop(0, slab // TOGETHER, near_step, 0)

    part[...] = jnp.zeros_like(part)

    def gram_step(i, carry):
        x = image[pl.ds(pl.multiple_of(i * 256, 256), 256)]
        part[...] += dot(x, x, 0, 0, HP).reshape(part.shape)
        return carry

    lax.fori_loop(0, slab * side // 256, gram_step, 0)

    first = []
    for d in range(1, reach):
        peer = lax.rem(r + d, reach)
        cp = remote(part.at[peer], buf1.at[d - 1], s1.at[d - 1], r1.at[d - 1], (z, peer))
        cp.start()
        first.append(cp)
    for cp in first:
        cp.wait()
    total = part[r]
    for d in range(reach - 1):
        total = total + buf1[d]
    quarter[...] = total
    second = []
    for d in range(1, rows):
        peer = lax.rem(z + d, rows)
        cp = remote(quarter, buf2.at[z], s2.at[d - 1], r2.at[d - 1], (peer, r))
        cp.start()
        second.append(cp)
    buf2[z] = total
    for cp in second:
        cp.wait()
    total = buf2[0]
    for d in range(1, rows):
        total = total + buf2[d]
    gram[r] = total
    third = []
    for d in range(1, reach):
        peer = lax.rem(r + d, reach)
        cp = remote(gram.at[r], gram.at[r], s3.at[d - 1], r3.at[d - 1], (z, peer))
        cp.start()
        third.append(cp)
    for cp in third:
        cp.wait()


def image_and_gram(
    rows,
    reach,
    basis,
    near_cols,
    near_count,
    near_blocks,
    marker_rows,
    marker_groups,
    marker_count,
    marker_weights,
    stiffness,
):
    slab, stored = near_cols.shape
    width = basis.shape[1]
    side = BS
    slots = marker_rows.shape[0]
    per = NG // (rows * reach)
    s = lax.axis_index(("row", "reach")).astype(jnp.int32)
    base = s * per
    away = lax.rem(base + NG // 2, NG)
    live = jnp.arange(stored, dtype=jnp.int32)[None, :] < near_count[:, None]
    cols = jnp.where(live, near_cols, reach * slab).reshape(-1)
    mlive = jnp.arange(slots, dtype=jnp.int32) < marker_count[0]
    code = jnp.where(
        marker_groups == base, 0, jnp.where(marker_groups == away, 1, 2)
    ).astype(jnp.int32)
    code = jnp.where(mlive, code, 3)
    blocks = near_blocks.reshape(slab, stored, side, side)
    weights = marker_weights.reshape(slots, side, side)
    st = stiffness.reshape(NG, side)
    stiff = jnp.stack(
        [lax.dynamic_index_in_dim(st, g, 0, keepdims=False) for g in (base, away, base + 1)]
    )[:, :, None]
    q = width // reach
    f32, bf16 = jnp.float32, jnp.bfloat16
    dma = pltpu.SemaphoreType.DMA
    image, gram = pl.pallas_call(
        functools.partial(image_kernel, rows, reach),
        out_shape=(
            jax.ShapeDtypeStruct((slab * side, width), f32),
            jax.ShapeDtypeStruct((reach, q, width), f32),
        ),
        in_specs=[SM, SM, SM, VM, VM, VM, VM],
        out_specs=(VM, VM),
        scratch_shapes=[
            pltpu.VMEM((reach * slab + 1, side, width), bf16),
            pltpu.VMEM((3, side, width), f32),
            pltpu.VMEM((2, side, width), f32),
            pltpu.VMEM((3, side, width), bf16),
            pltpu.VMEM((slots, side, width), f32),
            pltpu.VMEM((reach, q, width), f32),
            pltpu.VMEM((reach - 1, q, width), f32),
            pltpu.VMEM((q, width), f32),
            pltpu.VMEM((rows, q, width), f32),
            dma,
            dma,
            dma,
            dma((CHUNKS,)),
            dma((CHUNKS,)),
            dma((CHUNKS,)),
            dma((CHUNKS,)),
            dma,
            dma,
            dma((reach - 1,)),
            dma((reach - 1,)),
            dma((rows - 1,)),
            dma((rows - 1,)),
            dma((reach - 1,)),
            dma((reach - 1,)),
        ],
        compiler_params=pltpu.CompilerParams(
            collective_id=0, has_side_effects=True, vmem_limit_bytes=40 * 1024 * 1024
        ),
    )(
        cols,
        marker_rows,
        code,
        basis.reshape(slab, side, width),
        blocks,
        weights,
        stiff,
    )
    return image, gram.reshape(width, width)


def factor_kernel(root, image, gram, qf, rf, work, full):
    n = gram.shape[0]
    row = lax.broadcasted_iota(jnp.int32, (n, n), 0)
    col = lax.broadcasted_iota(jnp.int32, (n, n), 1)
    work[:, :n] = gram[...]
    work[:, n:] = jnp.where(row == col, 1.0, 0.0)
    sub = lax.broadcasted_iota(jnp.int32, (8, n), 0)
    for p in range(0, n, 8):
        left = work[p : p + 8, :n]
        right = work[p : p + 8, n:]
        cs = [jnp.broadcast_to(left[:, p + j : p + j + 1], (8, n)) for j in range(8)]
        scale = jnp.zeros((8, n), jnp.float32)
        for j in range(8):
            piv = cs[j][j : j + 1, :]
            rs = lax.rsqrt(piv)
            rs = rs * (1.5 - 0.5 * piv * rs * rs)
            scale = jnp.where(sub == j, rs, scale)
            if j == 7:
                break
            mult = jnp.where(sub > j, cs[j] * (rs * rs), 0.0)
            for i in range(j + 1, 8):
                cs[i] = cs[i] - mult * cs[i][j : j + 1, :]
            left = left - mult * left[j : j + 1, :]
            right = right - mult * right[j : j + 1, :]
        left = left * scale
        right = right * scale
        full[p : p + 8, :n] = left
        full[p : p + 8, n:] = right
        if p + 8 < n:
            both = jnp.concatenate([left, right], axis=1)
            change = dot(left, both, 0, 0, HP)
            work[p + 8 :, :] = work[p + 8 :, :] - change[p + 8 :, :]
    rf[...] = jnp.where(col >= row, full[:, :n], 0.0) * (1.0 / root)
    inverse = full[:, n:] * root

    def step(i, carry):
        at = pl.ds(pl.multiple_of(i * 256, 256), 256)
        qf[at] = dot(image[at], inverse, 1, 1, HP)
        return carry

    lax.fori_loop(0, image.shape[0] // 256, step, 0)


def factor(image, gram, total_rows):
    n = gram.shape[0]
    f32 = jnp.float32
    return pl.pallas_call(
        functools.partial(factor_kernel, float(total_rows) ** 0.5),
        out_shape=(
            jax.ShapeDtypeStruct(image.shape, f32),
            jax.ShapeDtypeStruct((n, n), f32),
        ),
        in_specs=[VM, VM],
        out_specs=(VM, VM),
        scratch_shapes=[pltpu.VMEM((n, 2 * n), f32), pltpu.VMEM((n, 2 * n), f32)],
        compiler_params=pltpu.CompilerParams(vmem_limit_bytes=40 * 1024 * 1024),
    )(image, gram)


def pick(index, table):
    count = table.shape[0]
    hot = index[:, None] == jnp.arange(count, dtype=jnp.int32)[None, :]
    taken = jnp.dot(hot.astype(table.dtype), table.reshape(count, -1))
    return taken.reshape((index.shape[0],) + table.shape[1:])


def plain_image_and_gram(
    basis,
    near_cols,
    near_count,
    near_blocks,
    marker_rows,
    marker_groups,
    marker_count,
    marker_weights,
    stiffness,
):
    slab, stored = near_cols.shape
    width = basis.shape[1]
    side = BS
    slots = marker_rows.shape[0]
    groups = NG
    own = basis.reshape(slab, side, width)
    weights = marker_weights.reshape(slots, side, side)
    mlive = jnp.arange(slots, dtype=jnp.int32) < marker_count[0]
    picked = pick(marker_rows, own)
    partial_value = jnp.einsum("mcj,mcd->mjd", weights, picked, preferred_element_type=jnp.float32)
    onehot = (marker_groups[None, :] == jnp.arange(groups, dtype=jnp.int32)[:, None]) & mlive[
        None, :
    ]
    sums = jnp.dot(
        onehot.astype(jnp.float32), partial_value.reshape(slots, side * width), precision=HP
    ).reshape(groups * side, width)
    sums = lax.psum(sums, ("row", "reach"))
    scale = lax.rsqrt(1.0 + jnp.mean(sums * sums, axis=1, keepdims=True))
    force = (stiffness[:, None] * sums * scale).astype(jnp.bfloat16)
    force_rows = jnp.dot(
        onehot.T.astype(jnp.bfloat16),
        force.reshape(groups, side * width),
        preferred_element_type=jnp.float32,
    )
    group_basis = lax.all_gather(basis, "reach", axis=0, tiled=True).reshape(-1, side, width)
    live = jnp.arange(stored, dtype=jnp.int32)[None, :] < near_count[:, None]
    fetched = pick(jnp.where(live, near_cols, -1).reshape(-1), group_basis)
    fetched = fetched.reshape(slab, stored, side, width)
    blocks = near_blocks.reshape(slab, stored, side, side)
    near = jnp.einsum("bkrc,bkcd->brd", blocks, fetched, preferred_element_type=jnp.float32)
    force_rows = force_rows.astype(jnp.bfloat16).reshape(slots, side, width)
    contrib = jnp.einsum("mcj,mjd->mcd", weights, force_rows, preferred_element_type=jnp.float32)
    rowhot = (
        (marker_rows[None, :] == jnp.arange(slab, dtype=jnp.int32)[:, None]) & mlive[None, :]
    ).astype(jnp.float32)
    spread = jnp.dot(rowhot, contrib.reshape(slots, side * width), precision=HP).reshape(
        slab, side, width
    )
    image = (near + spread).reshape(slab * side, width)
    gram = lax.psum(jnp.dot(image.T, image, precision=HP), ("row", "reach"))
    return image, gram


def solution(mesh):
    rows, reach = mesh.shape["row"], mesh.shape["reach"]
    devices = rows * reach
    paired = reach == 4 and rows % 2 == 0 and NG % devices == 0 and NG // devices >= 2

    def local(*args):
        if paired:
            image, gram = image_and_gram(rows, reach, *args)
        else:
            image, gram = plain_image_and_gram(*args)
        return factor(image, gram, image.shape[0] * devices)

    return jax.shard_map(
        local,
        mesh=mesh,
        in_specs=(
            P(("row", "reach"), None),
            P(("row", "reach"), None),
            P(("row", "reach")),
            P(("row", "reach"), None, None),
            P(("row", "reach")),
            P(("row", "reach")),
            P(("row", "reach")),
            P(("row", "reach"), None),
            P(),
        ),
        out_specs=(P(("row", "reach"), None), P()),
        check_vma=False,
    )
```

```python
import functools

import jax
import jax.numpy as jnp
from jax import lax
from jax.experimental import pallas as pl
from jax.experimental.pallas import tpu as pltpu
from jax.sharding import PartitionSpec as P

BS = 64
NG = 64
CHUNKS = 4
TOGETHER = 4
HP = lax.Precision.HIGHEST
MESH = pl.DeviceIdType.MESH
VM = pl.BlockSpec(memory_space=pltpu.VMEM)
SM = pl.BlockSpec(memory_space=pltpu.SMEM)


def dot(a, b, da, db, precision=None):
    return lax.dot_general(
        a, b, (((da,), (db,)), ((), ())), precision=precision, preferred_element_type=jnp.float32
    )


def image_kernel(
    rows,
    reach,
    cols,
    mrow,
    code,
    basis,
    blocks,
    weights,
    stiff,
    image,
    gram,
    held,
    held_sem,
    grp,
    sums,
    other,
    force,
    contrib,
    part,
    buf1,
    quarter,
    buf2,
    local_sem,
    sib_send,
    sib_recv,
    y_send,
    y_recv,
    f_send,
    f_recv,
    m_send,
    m_recv,
    s1,
    r1,
    s2,
    r2,
    s3,
    r3,
):
    z = lax.axis_index("row")
    r = lax.axis_index("reach")
    slab, side, width = basis.shape
    stored = blocks.shape[0]
    slots = weights.shape[0]
    core = lax.rem(r, 2)
    sib = r + 1 - 2 * core
    far = lax.rem(r + 2, reach)

    barrier = pltpu.get_barrier_semaphore()
    for d in range(1, reach):
        pl.semaphore_signal(
            barrier, inc=1, device_id=(z, lax.rem(r + d, reach)), device_id_type=MESH
        )
    for d in range(1, rows):
        pl.semaphore_signal(
            barrier, inc=1, device_id=(lax.rem(z + d, rows), r), device_id_type=MESH
        )
    pl.semaphore_wait(barrier, reach + rows - 2)

    def remote(src, dst, ss, rs, dev):
        return pltpu.make_async_remote_copy(
            src_ref=src, dst_ref=dst, send_sem=ss, recv_sem=rs, device_id=dev, device_id_type=MESH
        )

    step = slab // CHUNKS
    to_far = []
    for c in range(CHUNKS):
        cp = remote(
            basis.at[pl.ds(c * step, step)],
            grp.at[pl.ds(r * slab + c * step, step)],
            y_send.at[c],
            y_recv.at[c],
            (z, far),
        )
        cp.start()
        to_far.append(cp)
    to_sib = remote(basis, grp.at[pl.ds(r * slab, slab)], sib_send, sib_recv, (z, sib))
    to_sib.start()
    own = pltpu.make_async_copy(basis, grp.at[pl.ds(r * slab, slab)], local_sem)
    own.start()
    load = pltpu.make_async_copy(blocks, held, held_sem)
    load.start()
    grp[reach * slab] = jnp.zeros((side, width), grp.dtype)

    sums[...] = jnp.zeros_like(sums)

    def gather_step(t, carry):
        ms = [t * TOGETHER + u for u in range(TOGETHER)]
        values = [dot(weights[m], basis[mrow[m]], 0, 0) for m in ms]
        for g in range(3):
            total = sums[g]
            for m, value in zip(ms, values):
                total = total + jnp.where(code[m] == g, 1.0, 0.0) * value
            sums[g] = total
        return carry

    lax.fori_loop(0, slots // TOGETHER, gather_step, 0)
    swap = remote(
        sums.at[pl.ds(0, 2)], other, m_send, m_recv, (lax.rem(z + rows // 2, rows), r)
    )
    swap.start()

    def force_of(total, g):
        scale = lax.rsqrt(1.0 + jnp.mean(total * total, axis=1, keepdims=True))
        return (stiff[g] * total * scale).astype(jnp.bfloat16)

    force[2] = force_of(sums[2], 2)
    fwd = []
    for c in range(CHUNKS):
        to_far[c].wait_recv()
        place = pl.ds(far * slab + c * step, step)
        cp = remote(grp.at[place], grp.at[place], f_send.at[c], f_recv.at[c], (z, sib))
        cp.start()
        fwd.append(cp)
    swap.wait()
    force[0] = force_of(sums[0] + other[1], 0)
    force[1] = force_of(sums[1] + other[0], 1)

    def spread_step(t, carry):
        ms = [t * TOGETHER + u for u in range(TOGETHER)]
        values = [dot(weights[m], force[jnp.minimum(code[m], 2)], 1, 0) for m in ms]
        for m, value in zip(ms, values):
            contrib[m] = value
        return carry

    lax.fori_loop(0, slots // TOGETHER, spread_step, 0)

    own.wait()
    load.wait()
    to_sib.wait()
    for c in range(CHUNKS):
        to_far[c].wait_send()
        fwd[c].wait()

    def near_step(t, carry):
        lines = [t * TOGETHER + u for u in range(TOGETHER)]
        accs = [dot(held[0, i], grp[cols[i * stored]], 1, 0) for i in lines]
        for k in range(1, stored):
            accs = [
                acc + dot(held[k, i], grp[cols[i * stored + k]], 1, 0)
                for i, acc in zip(lines, accs)
            ]
        for m in range(slots):
            term = contrib[m]
            accs = [
                acc + jnp.where((mrow[m] == i) & (code[m] < 3), 1.0, 0.0) * term
                for i, acc in zip(lines, accs)
            ]
        for i, acc in zip(lines, accs):
            image[pl.ds(pl.multiple_of(i * side, side), side)] = acc
        return carry

    lax.fori_loop(0, slab // TOGETHER, near_step, 0)

    part[...] = jnp.zeros_like(part)

    def gram_step(i, carry):
        x = image[pl.ds(pl.multiple_of(i * 256, 256), 256)]
        part[...] += dot(x, x, 0, 0, HP).reshape(part.shape)
        return carry

    lax.fori_loop(0, slab * side // 256, gram_step, 0)

    first = []
    for d in range(1, reach):
        peer = lax.rem(r + d, reach)
        cp = remote(part.at[peer], buf1.at[d - 1], s1.at[d - 1], r1.at[d - 1], (z, peer))
        cp.start()
        first.append(cp)
    for cp in first:
        cp.wait()
    total = part[r]
    for d in range(reach - 1):
        total = total + buf1[d]
    quarter[...] = total
    second = []
    for d in range(1, rows):
        peer = lax.rem(z + d, rows)
        cp = remote(quarter, buf2.at[z], s2.at[d - 1], r2.at[d - 1], (peer, r))
        cp.start()
        second.append(cp)
    buf2[z] = total
    for cp in second:
        cp.wait()
    total = buf2[0]
    for d in range(1, rows):
        total = total + buf2[d]
    gram[r] = total
    third = []
    for d in range(1, reach):
        peer = lax.rem(r + d, reach)
        cp = remote(gram.at[r], gram.at[r], s3.at[d - 1], r3.at[d - 1], (z, peer))
        cp.start()
        third.append(cp)
    for cp in third:
        cp.wait()


def image_and_gram(
    rows,
    reach,
    basis,
    near_cols,
    near_count,
    near_blocks,
    marker_rows,
    marker_groups,
    marker_count,
    marker_weights,
    stiffness,
):
    slab, stored = near_cols.shape
    width = basis.shape[1]
    side = BS
    slots = marker_rows.shape[0]
    per = NG // (rows * reach)
    s = lax.axis_index(("row", "reach")).astype(jnp.int32)
    base = s * per
    away = lax.rem(base + NG // 2, NG)
    live = jnp.arange(stored, dtype=jnp.int32)[None, :] < near_count[:, None]
    cols = jnp.where(live, near_cols, reach * slab).reshape(-1)
    mlive = jnp.arange(slots, dtype=jnp.int32) < marker_count[0]
    code = jnp.where(
        marker_groups == base, 0, jnp.where(marker_groups == away, 1, 2)
    ).astype(jnp.int32)
    code = jnp.where(mlive, code, 3)
    blocks = near_blocks.reshape(slab, stored, side, side).transpose(1, 0, 2, 3)
    weights = marker_weights.reshape(slots, side, side)
    st = stiffness.reshape(NG, side)
    stiff = jnp.stack(
        [lax.dynamic_index_in_dim(st, g, 0, keepdims=False) for g in (base, away, base + 1)]
    )[:, :, None]
    q = width // reach
    f32, bf16 = jnp.float32, jnp.bfloat16
    dma = pltpu.SemaphoreType.DMA
    image, gram = pl.pallas_call(
        functools.partial(image_kernel, rows, reach),
        out_shape=(
            jax.ShapeDtypeStruct((slab * side, width), f32),
            jax.ShapeDtypeStruct((reach, q, width), f32),
        ),
        in_specs=[SM, SM, SM, VM, pl.BlockSpec(memory_space=pl.ANY), VM, VM],
        out_specs=(VM, VM),
        scratch_shapes=[
            pltpu.VMEM((stored, slab, side, side), bf16),
            dma,
            pltpu.VMEM((reach * slab + 1, side, width), bf16),
            pltpu.VMEM((3, side, width), f32),
            pltpu.VMEM((2, side, width), f32),
            pltpu.VMEM((3, side, width), bf16),
            pltpu.VMEM((slots, side, width), f32),
            pltpu.VMEM((reach, q, width), f32),
            pltpu.VMEM((reach - 1, q, width), f32),
            pltpu.VMEM((q, width), f32),
            pltpu.VMEM((rows, q, width), f32),
            dma,
            dma,
            dma,
            dma((CHUNKS,)),
            dma((CHUNKS,)),
            dma((CHUNKS,)),
            dma((CHUNKS,)),
            dma,
            dma,
            dma((reach - 1,)),
            dma((reach - 1,)),
            dma((rows - 1,)),
            dma((rows - 1,)),
            dma((reach - 1,)),
            dma((reach - 1,)),
        ],
        compiler_params=pltpu.CompilerParams(
            collective_id=0, has_side_effects=True, vmem_limit_bytes=56 * 1024 * 1024
        ),
    )(
        cols,
        marker_rows,
        code,
        basis.reshape(slab, side, width),
        blocks,
        weights,
        stiff,
    )
    return image, gram.reshape(width, width)


def factor_kernel(root, image, gram, qf, rf, work, full):
    n = gram.shape[0]
    row = lax.broadcasted_iota(jnp.int32, (n, n), 0)
    col = lax.broadcasted_iota(jnp.int32, (n, n), 1)
    work[:, :n] = gram[...]
    work[:, n:] = jnp.where(row == col, 1.0, 0.0)
    sub = lax.broadcasted_iota(jnp.int32, (8, n), 0)
    for p in range(0, n, 8):
        left = work[p : p + 8, :n]
        right = work[p : p + 8, n:]
        cs = [jnp.broadcast_to(left[:, p + j : p + j + 1], (8, n)) for j in range(8)]
        scale = jnp.zeros((8, n), jnp.float32)
        for j in range(8):
            piv = cs[j][j : j + 1, :]
            rs = lax.rsqrt(piv)
            rs = rs * (1.5 - 0.5 * piv * rs * rs)
            scale = jnp.where(sub == j, rs, scale)
            if j == 7:
                break
            mult = jnp.where(sub > j, cs[j] * (rs * rs), 0.0)
            for i in range(j + 1, 8):
                cs[i] = cs[i] - mult * cs[i][j : j + 1, :]
            left = left - mult * left[j : j + 1, :]
            right = right - mult * right[j : j + 1, :]
        left = left * scale
        right = right * scale
        full[p : p + 8, :n] = left
        full[p : p + 8, n:] = right
        if p + 8 < n:
            both = jnp.concatenate([left, right], axis=1)
            change = dot(left, both, 0, 0, HP)
            work[p + 8 :, :] = work[p + 8 :, :] - change[p + 8 :, :]
    rf[...] = jnp.where(col >= row, full[:, :n], 0.0) * (1.0 / root)
    inverse = full[:, n:] * root

    def step(i, carry):
        at = pl.ds(pl.multiple_of(i * 256, 256), 256)
        qf[at] = dot(image[at], inverse, 1, 1, HP)
        return carry

    lax.fori_loop(0, image.shape[0] // 256, step, 0)


def factor(image, gram, total_rows):
    n = gram.shape[0]
    f32 = jnp.float32
    return pl.pallas_call(
        functools.partial(factor_kernel, float(total_rows) ** 0.5),
        out_shape=(
            jax.ShapeDtypeStruct(image.shape, f32),
            jax.ShapeDtypeStruct((n, n), f32),
        ),
        in_specs=[VM, VM],
        out_specs=(VM, VM),
        scratch_shapes=[pltpu.VMEM((n, 2 * n), f32), pltpu.VMEM((n, 2 * n), f32)],
        compiler_params=pltpu.CompilerParams(vmem_limit_bytes=40 * 1024 * 1024),
    )(image, gram)


def pick(index, table):
    count = table.shape[0]
    hot = index[:, None] == jnp.arange(count, dtype=jnp.int32)[None, :]
    taken = jnp.dot(hot.astype(table.dtype), table.reshape(count, -1))
    return taken.reshape((index.shape[0],) + table.shape[1:])


def plain_image_and_gram(
    basis,
    near_cols,
    near_count,
    near_blocks,
    marker_rows,
    marker_groups,
    marker_count,
    marker_weights,
    stiffness,
):
    slab, stored = near_cols.shape
    width = basis.shape[1]
    side = BS
    slots = marker_rows.shape[0]
    groups = NG
    own = basis.reshape(slab, side, width)
    weights = marker_weights.reshape(slots, side, side)
    mlive = jnp.arange(slots, dtype=jnp.int32) < marker_count[0]
    picked = pick(marker_rows, own)
    partial_value = jnp.einsum("mcj,mcd->mjd", weights, picked, preferred_element_type=jnp.float32)
    onehot = (marker_groups[None, :] == jnp.arange(groups, dtype=jnp.int32)[:, None]) & mlive[
        None, :
    ]
    sums = jnp.dot(
        onehot.astype(jnp.float32), partial_value.reshape(slots, side * width), precision=HP
    ).reshape(groups * side, width)
    sums = lax.psum(sums, ("row", "reach"))
    scale = lax.rsqrt(1.0 + jnp.mean(sums * sums, axis=1, keepdims=True))
    force = (stiffness[:, None] * sums * scale).astype(jnp.bfloat16)
    force_rows = jnp.dot(
        onehot.T.astype(jnp.bfloat16),
        force.reshape(groups, side * width),
        preferred_element_type=jnp.float32,
    )
    group_basis = lax.all_gather(basis, "reach", axis=0, tiled=True).reshape(-1, side, width)
    live = jnp.arange(stored, dtype=jnp.int32)[None, :] < near_count[:, None]
    fetched = pick(jnp.where(live, near_cols, -1).reshape(-1), group_basis)
    fetched = fetched.reshape(slab, stored, side, width)
    blocks = near_blocks.reshape(slab, stored, side, side)
    near = jnp.einsum("bkrc,bkcd->brd", blocks, fetched, preferred_element_type=jnp.float32)
    force_rows = force_rows.astype(jnp.bfloat16).reshape(slots, side, width)
    contrib = jnp.einsum("mcj,mjd->mcd", weights, force_rows, preferred_element_type=jnp.float32)
    rowhot = (
        (marker_rows[None, :] == jnp.arange(slab, dtype=jnp.int32)[:, None]) & mlive[None, :]
    ).astype(jnp.float32)
    spread = jnp.dot(rowhot, contrib.reshape(slots, side * width), precision=HP).reshape(
        slab, side, width
    )
    image = (near + spread).reshape(slab * side, width)
    gram = lax.psum(jnp.dot(image.T, image, precision=HP), ("row", "reach"))
    return image, gram


def solution(mesh):
    rows, reach = mesh.shape["row"], mesh.shape["reach"]
    devices = rows * reach
    paired = reach == 4 and rows % 2 == 0 and NG % devices == 0 and NG // devices >= 2

    def local(*args):
        if paired:
            image, gram = image_and_gram(rows, reach, *args)
        else:
            image, gram = plain_image_and_gram(*args)
        return factor(image, gram, image.shape[0] * devices)

    return jax.shard_map(
        local,
        mesh=mesh,
        in_specs=(
            P(("row", "reach"), None),
            P(("row", "reach"), None),
            P(("row", "reach")),
            P(("row", "reach"), None, None),
            P(("row", "reach")),
            P(("row", "reach")),
            P(("row", "reach")),
            P(("row", "reach"), None),
            P(),
        ),
        out_specs=(P(("row", "reach"), None), P()),
        check_vma=False,
    )
```

```python
import functools

import jax
import jax.numpy as jnp
from jax import lax
from jax.experimental import pallas as pl
from jax.experimental.pallas import tpu as pltpu
from jax.sharding import PartitionSpec as P

BS = 64
NG = 64
CHUNKS = 4
TOGETHER = 4
HP = lax.Precision.HIGHEST
MESH = pl.DeviceIdType.MESH
VM = pl.BlockSpec(memory_space=pltpu.VMEM)
SM = pl.BlockSpec(memory_space=pltpu.SMEM)


def dot(a, b, da, db, precision=None):
    return lax.dot_general(
        a, b, (((da,), (db,)), ((), ())), precision=precision, preferred_element_type=jnp.float32
    )


def image_kernel(
    rows,
    reach,
    cols,
    mrow,
    code,
    basis,
    blocks,
    weights,
    stiff,
    image,
    gram,
    held,
    held_sem,
    grp,
    sums,
    other,
    force,
    contrib,
    part,
    buf1,
    quarter,
    buf2,
    local_sem,
    sib_send,
    sib_recv,
    y_send,
    y_recv,
    f_send,
    f_recv,
    m_send,
    m_recv,
    s1,
    r1,
    s2,
    r2,
    s3,
    r3,
):
    z = lax.axis_index("row")
    r = lax.axis_index("reach")
    slab, side, width = basis.shape
    stored = blocks.shape[0]
    slots = weights.shape[0]
    core = lax.rem(r, 2)
    sib = r + 1 - 2 * core
    far = lax.rem(r + 2, reach)

    barrier = pltpu.get_barrier_semaphore()
    for d in range(1, reach):
        pl.semaphore_signal(
            barrier, inc=1, device_id=(z, lax.rem(r + d, reach)), device_id_type=MESH
        )
    for d in range(1, rows):
        pl.semaphore_signal(
            barrier, inc=1, device_id=(lax.rem(z + d, rows), r), device_id_type=MESH
        )
    pl.semaphore_wait(barrier, reach + rows - 2)

    def remote(src, dst, ss, rs, dev):
        return pltpu.make_async_remote_copy(
            src_ref=src, dst_ref=dst, send_sem=ss, recv_sem=rs, device_id=dev, device_id_type=MESH
        )

    step = slab // CHUNKS
    to_far = []
    for c in range(CHUNKS):
        cp = remote(
            basis.at[pl.ds(c * step, step)],
            grp.at[pl.ds(r * slab + c * step, step)],
            y_send.at[c],
            y_recv.at[c],
            (z, far),
        )
        cp.start()
        to_far.append(cp)
    to_sib = remote(basis, grp.at[pl.ds(r * slab, slab)], sib_send, sib_recv, (z, sib))
    to_sib.start()
    own = pltpu.make_async_copy(basis, grp.at[pl.ds(r * slab, slab)], local_sem)
    own.start()
    load = pltpu.make_async_copy(blocks, held, held_sem)
    load.start()
    grp[reach * slab] = jnp.zeros((side, width), grp.dtype)

    sums[...] = jnp.zeros_like(sums)

    def gather_step(t, carry):
        ms = [t * TOGETHER + u for u in range(TOGETHER)]
        values = [dot(weights[m], basis[mrow[m]], 0, 0) for m in ms]
        for g in range(3):
            total = sums[g]
            for m, value in zip(ms, values):
                total = total + jnp.where(code[m] == g, 1.0, 0.0) * value
            sums[g] = total
        return carry

    lax.fori_loop(0, slots // TOGETHER, gather_step, 0)
    swap = remote(
        sums.at[pl.ds(0, 2)], other, m_send, m_recv, (lax.rem(z + rows // 2, rows), r)
    )
    swap.start()

    def force_of(total, g):
        scale = lax.rsqrt(1.0 + jnp.mean(total * total, axis=1, keepdims=True))
        return (stiff[g] * total * scale).astype(jnp.bfloat16)

    force[2] = force_of(sums[2], 2)
    fwd = []
    for c in range(CHUNKS):
        to_far[c].wait_recv()
        place = pl.ds(far * slab + c * step, step)
        cp = remote(grp.at[place], grp.at[place], f_send.at[c], f_recv.at[c], (z, sib))
        cp.start()
        fwd.append(cp)
    swap.wait()
    force[0] = force_of(sums[0] + other[1], 0)
    force[1] = force_of(sums[1] + other[0], 1)

    def spread_step(t, carry):
        ms = [t * TOGETHER + u for u in range(TOGETHER)]
        values = [dot(weights[m], force[jnp.minimum(code[m], 2)], 1, 0) for m in ms]
        for m, value in zip(ms, values):
            contrib[m] = value
        return carry

    lax.fori_loop(0, slots // TOGETHER, spread_step, 0)

    own.wait()
    load.wait()
    to_sib.wait()
    for c in range(CHUNKS):
        to_far[c].wait_send()
        fwd[c].wait()

    def near_step(t, carry):
        lines = [t * TOGETHER + u for u in range(TOGETHER)]
        accs = [dot(held[0, i], grp[cols[i * stored]], 1, 0) for i in lines]
        for k in range(1, stored):
            accs = [
                acc + dot(held[k, i], grp[cols[i * stored + k]], 1, 0)
                for i, acc in zip(lines, accs)
            ]
        for m in range(slots):
            term = contrib[m]
            accs = [
                acc + jnp.where((mrow[m] == i) & (code[m] < 3), 1.0, 0.0) * term
                for i, acc in zip(lines, accs)
            ]
        for i, acc in zip(lines, accs):
            image[pl.ds(pl.multiple_of(i * side, side), side)] = acc
        return carry

    lax.fori_loop(0, slab // TOGETHER, near_step, 0)

    part[...] = jnp.zeros_like(part)

    def gram_step(i, carry):
        x = image[pl.ds(pl.multiple_of(i * 256, 256), 256)]
        part[...] += dot(x, x, 0, 0, HP).reshape(part.shape)
        return carry

    lax.fori_loop(0, slab * side // 256, gram_step, 0)

    first = []
    for d in range(1, reach):
        peer = lax.rem(r + d, reach)
        cp = remote(part.at[peer], buf1.at[d - 1], s1.at[d - 1], r1.at[d - 1], (z, peer))
        cp.start()
        first.append(cp)
    for cp in first:
        cp.wait()
    total = part[r]
    for d in range(reach - 1):
        total = total + buf1[d]
    quarter[...] = total
    second = []
    for d in range(1, rows):
        peer = lax.rem(z + d, rows)
        cp = remote(quarter, buf2.at[z], s2.at[d - 1], r2.at[d - 1], (peer, r))
        cp.start()
        second.append(cp)
    buf2[z] = total
    for cp in second:
        cp.wait()
    total = buf2[0]
    for d in range(1, rows):
        total = total + buf2[d]
    gram[r] = total
    third = []
    for d in range(1, reach):
        peer = lax.rem(r + d, reach)
        cp = remote(gram.at[r], gram.at[r], s3.at[d - 1], r3.at[d - 1], (z, peer))
        cp.start()
        third.append(cp)
    for cp in third:
        cp.wait()


def image_and_gram(
    rows,
    reach,
    basis,
    near_cols,
    near_count,
    near_blocks,
    marker_rows,
    marker_groups,
    marker_count,
    marker_weights,
    stiffness,
):
    slab, stored = near_cols.shape
    width = basis.shape[1]
    side = BS
    slots = marker_rows.shape[0]
    per = NG // (rows * reach)
    s = lax.axis_index(("row", "reach")).astype(jnp.int32)
    base = s * per
    away = lax.rem(base + NG // 2, NG)
    live = jnp.arange(stored, dtype=jnp.int32)[None, :] < near_count[:, None]
    cols = jnp.where(live, near_cols, reach * slab).reshape(-1)
    mlive = jnp.arange(slots, dtype=jnp.int32) < marker_count[0]
    code = jnp.where(
        marker_groups == base, 0, jnp.where(marker_groups == away, 1, 2)
    ).astype(jnp.int32)
    code = jnp.where(mlive, code, 3)
    blocks = near_blocks.reshape(slab, stored, side, side).transpose(1, 0, 2, 3)
    weights = marker_weights.reshape(slots, side, side)
    st = stiffness.reshape(NG, side)
    stiff = jnp.stack(
        [lax.dynamic_index_in_dim(st, g, 0, keepdims=False) for g in (base, away, base + 1)]
    )[:, :, None]
    q = width // reach
    f32, bf16 = jnp.float32, jnp.bfloat16
    dma = pltpu.SemaphoreType.DMA
    image, gram = pl.pallas_call(
        functools.partial(image_kernel, rows, reach),
        out_shape=(
            jax.ShapeDtypeStruct((slab * side, width), f32),
            jax.ShapeDtypeStruct((reach, q, width), f32),
        ),
        in_specs=[SM, SM, SM, VM, pl.BlockSpec(memory_space=pl.ANY), VM, VM],
        out_specs=(VM, VM),
        scratch_shapes=[
            pltpu.VMEM((stored, slab, side, side), bf16),
            dma,
            pltpu.VMEM((reach * slab + 1, side, width), bf16),
            pltpu.VMEM((3, side, width), f32),
            pltpu.VMEM((2, side, width), f32),
            pltpu.VMEM((3, side, width), bf16),
            pltpu.VMEM((slots, side, width), f32),
            pltpu.VMEM((reach, q, width), f32),
            pltpu.VMEM((reach - 1, q, width), f32),
            pltpu.VMEM((q, width), f32),
            pltpu.VMEM((rows, q, width), f32),
            dma,
            dma,
            dma,
            dma((CHUNKS,)),
            dma((CHUNKS,)),
            dma((CHUNKS,)),
            dma((CHUNKS,)),
            dma,
            dma,
            dma((reach - 1,)),
            dma((reach - 1,)),
            dma((rows - 1,)),
            dma((rows - 1,)),
            dma((reach - 1,)),
            dma((reach - 1,)),
        ],
        compiler_params=pltpu.CompilerParams(
            collective_id=0, has_side_effects=True, vmem_limit_bytes=40 * 1024 * 1024
        ),
    )(
        cols,
        marker_rows,
        code,
        basis.reshape(slab, side, width),
        blocks,
        weights,
        stiff,
    )
    return image, gram.reshape(width, width)


def factor_kernel(root, image, gram, qf, rf, work, full):
    n = gram.shape[0]
    row = lax.broadcasted_iota(jnp.int32, (n, n), 0)
    col = lax.broadcasted_iota(jnp.int32, (n, n), 1)
    work[:, :n] = gram[...]
    work[:, n:] = jnp.where(row == col, 1.0, 0.0)
    sub = lax.broadcasted_iota(jnp.int32, (8, n), 0)
    for p in range(0, n, 8):
        left = work[p : p + 8, :n]
        right = work[p : p + 8, n:]
        cs = [jnp.broadcast_to(left[:, p + j : p + j + 1], (8, n)) for j in range(8)]
        scale = jnp.zeros((8, n), jnp.float32)
        for j in range(8):
            piv = cs[j][j : j + 1, :]
            rs = lax.rsqrt(piv)
            rs = rs * (1.5 - 0.5 * piv * rs * rs)
            scale = jnp.where(sub == j, rs, scale)
            if j == 7:
                break
            mult = jnp.where(sub > j, cs[j] * (rs * rs), 0.0)
            for i in range(j + 1, 8):
                cs[i] = cs[i] - mult * cs[i][j : j + 1, :]
            left = left - mult * left[j : j + 1, :]
            right = right - mult * right[j : j + 1, :]
        left = left * scale
        right = right * scale
        full[p : p + 8, :n] = left
        full[p : p + 8, n:] = right
        if p + 8 < n:
            both = jnp.concatenate([left, right], axis=1)
            change = dot(left, both, 0, 0, HP)
            work[p + 8 :, :] = work[p + 8 :, :] - change[p + 8 :, :]
    rf[...] = jnp.where(col >= row, full[:, :n], 0.0) * (1.0 / root)
    inverse = full[:, n:] * root

    def step(i, carry):
        at = pl.ds(pl.multiple_of(i * 256, 256), 256)
        qf[at] = dot(image[at], inverse, 1, 1, HP)
        return carry

    lax.fori_loop(0, image.shape[0] // 256, step, 0)


def factor(image, gram, total_rows):
    n = gram.shape[0]
    f32 = jnp.float32
    return pl.pallas_call(
        functools.partial(factor_kernel, float(total_rows) ** 0.5),
        out_shape=(
            jax.ShapeDtypeStruct(image.shape, f32),
            jax.ShapeDtypeStruct((n, n), f32),
        ),
        in_specs=[VM, VM],
        out_specs=(VM, VM),
        scratch_shapes=[pltpu.VMEM((n, 2 * n), f32), pltpu.VMEM((n, 2 * n), f32)],
        compiler_params=pltpu.CompilerParams(vmem_limit_bytes=40 * 1024 * 1024),
    )(image, gram)


def pick(index, table):
    count = table.shape[0]
    hot = index[:, None] == jnp.arange(count, dtype=jnp.int32)[None, :]
    taken = jnp.dot(hot.astype(table.dtype), table.reshape(count, -1))
    return taken.reshape((index.shape[0],) + table.shape[1:])


def plain_image_and_gram(
    basis,
    near_cols,
    near_count,
    near_blocks,
    marker_rows,
    marker_groups,
    marker_count,
    marker_weights,
    stiffness,
):
    slab, stored = near_cols.shape
    width = basis.shape[1]
    side = BS
    slots = marker_rows.shape[0]
    groups = NG
    own = basis.reshape(slab, side, width)
    weights = marker_weights.reshape(slots, side, side)
    mlive = jnp.arange(slots, dtype=jnp.int32) < marker_count[0]
    picked = pick(marker_rows, own)
    partial_value = jnp.einsum("mcj,mcd->mjd", weights, picked, preferred_element_type=jnp.float32)
    onehot = (marker_groups[None, :] == jnp.arange(groups, dtype=jnp.int32)[:, None]) & mlive[
        None, :
    ]
    sums = jnp.dot(
        onehot.astype(jnp.float32), partial_value.reshape(slots, side * width), precision=HP
    ).reshape(groups * side, width)
    sums = lax.psum(sums, ("row", "reach"))
    scale = lax.rsqrt(1.0 + jnp.mean(sums * sums, axis=1, keepdims=True))
    force = (stiffness[:, None] * sums * scale).astype(jnp.bfloat16)
    force_rows = jnp.dot(
        onehot.T.astype(jnp.bfloat16),
        force.reshape(groups, side * width),
        preferred_element_type=jnp.float32,
    )
    group_basis = lax.all_gather(basis, "reach", axis=0, tiled=True).reshape(-1, side, width)
    live = jnp.arange(stored, dtype=jnp.int32)[None, :] < near_count[:, None]
    fetched = pick(jnp.where(live, near_cols, -1).reshape(-1), group_basis)
    fetched = fetched.reshape(slab, stored, side, width)
    blocks = near_blocks.reshape(slab, stored, side, side)
    near = jnp.einsum("bkrc,bkcd->brd", blocks, fetched, preferred_element_type=jnp.float32)
    force_rows = force_rows.astype(jnp.bfloat16).reshape(slots, side, width)
    contrib = jnp.einsum("mcj,mjd->mcd", weights, force_rows, preferred_element_type=jnp.float32)
    rowhot = (
        (marker_rows[None, :] == jnp.arange(slab, dtype=jnp.int32)[:, None]) & mlive[None, :]
    ).astype(jnp.float32)
    spread = jnp.dot(rowhot, contrib.reshape(slots, side * width), precision=HP).reshape(
        slab, side, width
    )
    image = (near + spread).reshape(slab * side, width)
    gram = lax.psum(jnp.dot(image.T, image, precision=HP), ("row", "reach"))
    return image, gram


def solution(mesh):
    rows, reach = mesh.shape["row"], mesh.shape["reach"]
    devices = rows * reach
    paired = reach == 4 and rows % 2 == 0 and NG % devices == 0 and NG // devices >= 2

    def local(*args):
        if paired:
            image, gram = image_and_gram(rows, reach, *args)
        else:
            image, gram = plain_image_and_gram(*args)
        return factor(image, gram, image.shape[0] * devices)

    return jax.shard_map(
        local,
        mesh=mesh,
        in_specs=(
            P(("row", "reach"), None),
            P(("row", "reach"), None),
            P(("row", "reach")),
            P(("row", "reach"), None, None),
            P(("row", "reach")),
            P(("row", "reach")),
            P(("row", "reach")),
            P(("row", "reach"), None),
            P(),
        ),
        out_specs=(P(("row", "reach"), None), P()),
        check_vma=False,
    )
```
